32 devices in a mesh: row: 8 (over z, x), col: 4 (over y, core).
Axes of the slice: x: 2, y: 2, z: 4, core: 2. Of those that a mesh axis runs over, the one named last changes fastest.
Arguments:
- pole_values: float32 [16384], P('row'), may hold values from 0.3 to 127.9, as said below
- rank_one: float32 [16384], P('row'), may hold values from -6 to 6
- deflated: int32 [16384], P('row'), may hold values 0 or 1
- onsite_energy: float32 [16384], P('row'), may hold values from 0.5 to 3
- secular_roots: float32 [16, 256], replicated, may hold values from 0 to 127.7, as said below
- column_order: int32 [16, 256], replicated, may hold values from 0 to 255, each once within a row
- q_blocks: bfloat16 [32, 512, 512], P('row'), may hold values from -1 to 1, as said below
- diag_blocks: float32 [32, 512, 512], P('row'), may hold values from -0.15625 to 0.15625
- coupling_blocks: float32 [32, 512, 512], P('row'), may hold values from -0.15625 to 0.15625
Outputs:
- refined_panel: float32 [16, 16384, 256], P(None, 'row', 'col')
- new_roots: float32 [16, 256], P(None, 'col')
The draws below stay inside these ranges and needn't reach their ends.
Inputs may be any that keep to these rules, and one draw needn't show every extreme that they name: `pole_values`: every pole lies 0.3 to 0.4 above a multiple of 0.5, at most 0.5 * 256 - 0.1. `secular_roots`: the root of index j in a panel lies between 0.5 j and 0.5 j + 0.2. `q_blocks`: each block is an orthogonal matrix rounded to bfloat16.
All inputs are finite; a program needn't handle non-finite values. No bound on the sum of `deflated` on one device may be relied on, other than what follows from the above.
Results may differ from the reference program's by a relative error of at most 0.0004.
The reference program's roundings to bfloat16 on the way (of `scaled` and `formed`) count: a program that leaves them out, or rounds other values in their place, can miss the bound.
Values may be sent and summed in bfloat16 or wider, within the bound.
A program may use at most 192 MiB of HBM per device.

```python
import jax
import jax.numpy as jnp
from jax import lax

BLOCK = 512
PANEL = 256
PANELS = 16
NBLK = 32
N = 16384


def draw_pole_values(key, part):
    first_key, second_key = jax.random.split(jax.random.fold_in(key, 11))
    bins = jax.random.randint(first_key, (N,), 0, PANEL)
    offsets = jax.random.uniform(second_key, (N,), jnp.float32)
    return 0.5 * bins.astype(jnp.float32) + 0.3 + 0.1 * offsets


def draw_secular_roots(key, part):
    shifts = jax.random.uniform(jax.random.fold_in(key, 23), (PANELS, PANEL), jnp.float32)
    positions = jnp.arange(PANEL, dtype=jnp.float32)
    return 0.5 * positions[None, :] + 0.2 * shifts


def draw_q_blocks(key, part):
    gaussian = jax.random.normal(jax.random.fold_in(key, 37), (NBLK, BLOCK, BLOCK), jnp.float32)
    orthogonal, upper = jnp.linalg.qr(gaussian)
    return orthogonal.astype(jnp.bfloat16)


def touch_ends(drawn, key, low, largest):
    longest = drawn.shape.index(max(drawn.shape))
    spots = []
    for shift in (0, 1):
        where = [jax.random.randint(jax.random.fold_in(key, axis), (), 0, length) for axis, length in enumerate(drawn.shape)]
        where[longest] = (where[longest] + shift) % drawn.shape[longest]
        spots.append(tuple(where))
    return drawn.at[spots[0]].set(low).at[spots[1]].set(largest)


def shard_levels(key, dims, shards, smallest, largest):
    loudness = 1.0
    for axis_at, parts in shards:
        steps = jax.random.uniform(jax.random.fold_in(jax.random.fold_in(key, 6), axis_at), (parts,), jnp.float32, smallest / len(shards), largest / len(shards))
        loudness = loudness * jnp.repeat(jnp.exp(steps), dims[axis_at] // parts).reshape((-1,) + (1,) * (len(dims) - 1 - axis_at))
    return loudness


def scatter_about(own_key, extent, width, most, pieces=(), kind=jnp.bfloat16):
    loudness = shard_levels(own_key, extent, pieces, -0.22, 0.18) if pieces else 1.0
    entries = jax.random.normal(own_key, extent, jnp.float32) * width * loudness
    return jnp.minimum(jnp.maximum(entries, -most), most).astype(kind)


def setup_inputs(seed: int = 0) -> dict:
    key_of = jax.random.split(jax.random.key(seed), 10)
    pole_values = draw_pole_values(jax.random.fold_in(key_of[9], 71), 0)
    rank_one = scatter_about(key_of[1], (N,), 1.0, 6.0, ((0, 8),), jnp.float32)
    deflated = touch_ends((jax.random.randint(key_of[2], (N,), 0, 8) < 1).astype(jnp.int32), jax.random.fold_in(key_of[2], 1), 0, 1)
    onsite_energy = jnp.clip(0.5 + 2.5 * jax.random.uniform(key_of[3], (N,), jnp.float32) ** shard_levels(key_of[3], (N,), ((0, 8),), -0.2, 0.2), 0.5, 3.0)
    secular_roots = draw_secular_roots(jax.random.fold_in(key_of[9], 71), 0)
    column_order = jax.vmap(lambda own: jax.random.permutation(own, PANEL))(jax.random.split(key_of[5], PANELS)).reshape((PANELS, PANEL)).astype(jnp.int32)
    q_blocks = draw_q_blocks(jax.random.fold_in(key_of[9], 71), 0)
    diag_blocks = scatter_about(key_of[7], (NBLK, BLOCK, BLOCK), (3 * BLOCK) ** -0.5, 0.15625, ((0, 8),), jnp.float32)
    coupling_blocks = scatter_about(key_of[8], (NBLK, BLOCK, BLOCK), (3 * BLOCK) ** -0.5, 0.15625, ((0, 8),), jnp.float32)
    return dict(pole_values=pole_values, rank_one=rank_one, deflated=deflated, onsite_energy=onsite_energy, secular_roots=secular_roots, column_order=column_order, q_blocks=q_blocks, diag_blocks=diag_blocks, coupling_blocks=coupling_blocks)


EPSILON = 1e-06
HIGHEST = lax.Precision.HIGHEST

def reference(pole_values, rank_one, deflated, onsite_energy, secular_roots, column_order, q_blocks, diag_blocks, coupling_blocks):
    weights = rank_one * (1 - deflated).astype(jnp.float32)
    symmetric = 0.5 * (diag_blocks + jnp.swapaxes(diag_blocks, 1, 2))
    block_count = q_blocks.shape[0]
    block_size = q_blocks.shape[1]
    q_float = q_blocks.astype(jnp.float32)
    upper_blocks = jnp.concatenate([coupling_blocks[1:], jnp.zeros_like(coupling_blocks[:1])], axis=0)
    onsite_blocks = onsite_energy.reshape(block_count, block_size)

    def one_panel(inputs):
        roots_row, order_row = inputs
        chosen = roots_row[order_row]
        panel_size = chosen.shape[0]
        cauchy = weights[:, None] / (pole_values[:, None] - chosen[None, :])
        column_squares = lax.optimization_barrier(jnp.sum(cauchy * cauchy, axis=0))
        scaled = (cauchy * lax.rsqrt(column_squares + EPSILON)[None, :]).astype(jnp.bfloat16)
        blocked = scaled.astype(jnp.float32).reshape(block_count, block_size, panel_size)
        formed = jnp.einsum('bij,bjc->bic', q_float, blocked, precision=HIGHEST).astype(jnp.bfloat16)
        middle = formed.astype(jnp.float32)
        zero_block = jnp.zeros_like(middle[:1])
        lower_rows = jnp.concatenate([zero_block, middle[:-1]], axis=0)
        upper_rows = jnp.concatenate([middle[1:], zero_block], axis=0)
        operated = jnp.einsum('bij,bjc->bic', symmetric, middle, precision=HIGHEST)
        operated = operated + jnp.einsum('bij,bjc->bic', coupling_blocks, lower_rows, precision=HIGHEST)
        operated = operated + jnp.einsum('bji,bjc->bic', upper_blocks, upper_rows, precision=HIGHEST)
        operated = operated + onsite_blocks[:, :, None] * middle
        flat_rows = middle.reshape(-1, panel_size)
        flat_image = operated.reshape(-1, panel_size)
        gram = jnp.dot(flat_rows.T, flat_rows, precision=HIGHEST)
        projected = jnp.dot(flat_rows.T, flat_image, precision=HIGHEST)
        identity_mask = jnp.eye(panel_size, dtype=bool)
        residual = identity_mask.astype(jnp.float32) - gram
        spacing = chosen[None, :] - chosen[:, None] + identity_mask.astype(jnp.float32)
        update = jnp.where(identity_mask, 0.5 * residual, (projected + chosen[None, :] * residual) / spacing)
        updated = flat_rows + jnp.dot(flat_rows, update, precision=HIGHEST)
        column_sums = lax.optimization_barrier(jnp.sum(updated * updated, axis=0))
        refined = updated * jnp.sqrt(N / column_sums)[None, :]
        return (refined, jnp.diagonal(projected) / jnp.diagonal(gram))
    refined_panel, new_roots = lax.map(one_panel, (secular_roots, column_order))
    return (refined_panel, new_roots)
```

```python
import functools

import jax
import jax.numpy as jnp
from jax import lax
from jax.experimental import pallas as pl
from jax.experimental.pallas import tpu as pltpu
from jax.sharding import PartitionSpec as P

EPSILON = 1e-06
HIGHEST = lax.Precision.HIGHEST
MESH = pl.DeviceIdType.MESH
LANES = 128


def dot_nt(a, b):
    return lax.dot_general(a, b, (((1,), (1,)), ((), ())), preferred_element_type=jnp.float32)


def split(x):
    high = x.astype(jnp.bfloat16)
    return high, (x - high.astype(jnp.float32)).astype(jnp.bfloat16)


def widen(x, width):
    return jnp.concatenate([x] * (width // x.shape[1]), axis=1)


def column_form(row):
    return jnp.transpose(jnp.broadcast_to(row, (LANES, row.shape[1])))


def merge_kernel(
    rows,
    cols,
    pole_ref,
    rank_ref,
    defl_ref,
    onsite_ref,
    chosen_ref,
    chosen_col_ref,
    q_ref,
    diag_ref,
    coup_ref,
    formed_hbm,
    update_out,
    pw,
    halo_pw,
    halo_q,
    sq_send,
    sq_slots,
    factor_col,
    hmat,
    formed,
    halo,
    sums_send,
    sums_slots,
    v_full,
    v_send,
    out_sem,
    halo_send_sem,
    halo_recv_sem,
    sq_send_sem,
    sq_recv_sem,
    sums_send_sem,
    sums_recv_sem,
    v_send_sem,
    v_recv_sem,
):
    row = lax.axis_index("row")
    col = lax.axis_index("col")
    me = row * cols + col
    total = rows * cols
    panels, size = chosen_ref.shape
    own = panels // cols
    block_count, block, _ = q_ref.shape
    here = block_count * block
    width = size // cols
    spread = rows // own

    barrier = pltpu.get_barrier_semaphore()

    def greet(step, carry):
        other = lax.rem(me + step, total)
        pl.semaphore_signal(
            barrier, inc=1, device_id=(other // cols, lax.rem(other, cols)), device_id_type=MESH
        )
        return carry

    lax.fori_loop(1, total, greet, 0)

    weights = rank_ref[...] * (1 - defl_ref[...]).astype(jnp.float32)
    pw[0:8, :] = jnp.broadcast_to(pole_ref[...], (8, here))
    pw[8:16, :] = jnp.broadcast_to(weights, (8, here))

    def cauchy_of(poles, weight_row, panel):
        chosen = widen(chosen_col_ref[panel], poles.shape[1])
        return weight_row / (poles - chosen)

    sq_send[...] = jnp.zeros_like(sq_send)
    for k in range(own):

        def add_squares(b, acc):
            lanes = pl.ds(pl.multiple_of(b * block, block), block)
            c = cauchy_of(pw[0:1, lanes], pw[8:9, lanes], col * own + k)
            c = c * c
            for t in range(block // LANES):
                acc = acc + c[:, t * LANES : (t + 1) * LANES]
            return acc

        acc = lax.fori_loop(0, block_count, add_squares, jnp.zeros((size, LANES), jnp.float32))
        sq_send[k : k + 1, :] = jnp.sum(jnp.transpose(acc), axis=0, keepdims=True)

    pl.semaphore_wait(barrier, total - 1)

    last = block_count - 1
    tail = pl.ds(here - block, block)
    halo_copies = [
        pltpu.make_async_remote_copy(
            src_ref=source,
            dst_ref=target,
            send_sem=halo_send_sem.at[n],
            recv_sem=halo_recv_sem.at[n],
            device_id=(lax.rem(row + 1, rows), col),
            device_id_type=MESH,
        )
        for n, (source, target) in enumerate(((q_ref.at[last], halo_q), (pw.at[:, tail], halo_pw)))
    ]

    def square_copy(step):
        other = lax.rem(me + step, total)
        return pltpu.make_async_remote_copy(
            src_ref=sq_send,
            dst_ref=sq_slots.at[me],
            send_sem=sq_send_sem.at[step],
            recv_sem=sq_recv_sem.at[me],
            device_id=(other // cols, lax.rem(other, cols)),
            device_id_type=MESH,
        )

    def send_squares(step, carry):
        square_copy(step).start()
        return carry

    lax.fori_loop(1, total, send_squares, 0)

    @pl.when(row < rows - 1)
    def _():
        for copy in halo_copies:
            copy.start()

    sq_slots[me] = sq_send[...]

    for b in range(block_count):
        for n, part in enumerate((coup_ref[b], 0.5 * diag_ref[b])):
            high, low = split(part)
            hmat[b, n, 0] = high
            hmat[b, n, 1] = low

    def await_squares(step, carry):
        other = lax.rem(me + step, total)
        square_copy(step).wait_send()
        pltpu.make_async_remote_copy(
            src_ref=sq_send,
            dst_ref=sq_slots.at[other],
            send_sem=sq_send_sem.at[step],
            recv_sem=sq_recv_sem.at[other],
            device_id=(other // cols, lax.rem(other, cols)),
            device_id_type=MESH,
        ).wait_recv()
        return carry

    lax.fori_loop(1, total, await_squares, 0)

    for c in range(cols):
        sums = lax.fori_loop(
            0, rows, lambda r, a: a + sq_slots[r * cols + c], jnp.zeros(sq_send.shape, jnp.float32)
        )
        factor = lax.rsqrt(sums + EPSILON)
        for k in range(own):
            factor_col[c * own + k] = column_form(factor[k : k + 1, :])

    def form_block(poles, weight_row, panel, q_block):
        scaled = cauchy_of(poles, weight_row, panel) * widen(factor_col[panel], block)
        return dot_nt(scaled.astype(jnp.bfloat16), q_block).astype(jnp.bfloat16)

    def form_panel(panel):
        for b in range(block_count):
            lanes = pl.ds(b * block, block)
            formed[panel, :, lanes] = form_block(pw[0:1, lanes], pw[8:9, lanes], panel, q_ref[b])
        out_copy(panel).start()

    def out_copy(panel):
        return pltpu.make_async_copy(formed.at[panel], formed_hbm.at[panel], out_sem.at[panel])

    i_at = lax.broadcasted_iota(jnp.int32, (size, size), 0)
    j_at = lax.broadcasted_iota(jnp.int32, (size, size), 1)

    @pl.when(row > 0)
    def _():
        for copy in halo_copies:
            copy.wait_recv()

    def owner_row(k):
        return k * spread + lax.rem(col, spread)

    def sums_copy(k):
        return pltpu.make_async_remote_copy(
            src_ref=sums_send.at[k],
            dst_ref=sums_slots.at[row],
            send_sem=sums_send_sem.at[k],
            recv_sem=sums_recv_sem.at[row],
            device_id=(owner_row(k), col),
            device_id_type=MESH,
        )

    def own_panel(k, carry):
        panel = col * own + k
        form_panel(panel)

        @pl.when(row > 0)
        def _():
            halo[...] = form_block(halo_pw[0:1, :], halo_pw[8:9, :], panel, halo_q[...])

        @pl.when(row == 0)
        def _():
            halo[...] = jnp.zeros_like(halo)

        gram = jnp.zeros((size, size), jnp.float32)
        half = jnp.zeros((size, size), jnp.float32)
        for b in range(block_count):
            lanes = pl.ds(b * block, block)
            now = formed[panel, :, lanes]
            before = halo[...] if b == 0 else formed[panel, :, pl.ds((b - 1) * block, block)]
            image = dot_nt(before, hmat[b, 0, 0]) + dot_nt(before, hmat[b, 0, 1])
            image = image + dot_nt(now, hmat[b, 1, 0]) + dot_nt(now, hmat[b, 1, 1])
            image = image + 0.5 * onsite_ref[0:1, lanes] * now.astype(jnp.float32)
            high, low = split(image)
            gram = gram + dot_nt(now, now)
            half = half + dot_nt(now, high) + dot_nt(now, low)
        projected = half + jnp.transpose(half)
        sums_send[k, 0:size, :] = jnp.where(j_at > i_at, gram, projected)
        diagonal = jnp.sum(jnp.where(i_at == j_at, gram, 0.0), axis=0, keepdims=True)
        sums_send[k, size : size + 8, :] = jnp.broadcast_to(diagonal, (8, size))

        @pl.when(owner_row(k) != row)
        def _():
            sums_copy(k).start()

        @pl.when(owner_row(k) == row)
        def _():
            sums_slots[row] = sums_send[k]

        return carry

    lax.fori_loop(0, own, own_panel, 0)

    def rest(n, carry):
        form_panel(lax.rem(col * own + own + n, panels))
        return carry

    lax.fori_loop(0, panels - own, rest, 0)

    mine = row // spread
    owns = owner_row(mine) == row

    def update_copy(step):
        other = lax.rem(me + step, total)
        other_col = lax.rem(other, cols)
        return pltpu.make_async_remote_copy(
            src_ref=v_send.at[other_col],
            dst_ref=update_out.at[col * own + mine],
            send_sem=v_send_sem.at[step],
            recv_sem=v_recv_sem.at[col * own + mine],
            device_id=(other // cols, other_col),
            device_id_type=MESH,
        )

    @pl.when(owns)
    def _():
        panel = col * own + mine

        def arrive(step, carry):
            other = lax.rem(row + step, rows)
            pltpu.make_async_remote_copy(
                src_ref=sums_send.at[0],
                dst_ref=sums_slots.at[other],
                send_sem=sums_send_sem.at[0],
                recv_sem=sums_recv_sem.at[other],
                device_id=(other, col),
                device_id_type=MESH,
            ).wait_recv()
            return carry

        lax.fori_loop(1, rows, arrive, 0)
        sums = lax.fori_loop(
            1, rows, lambda r, a: a + sums_slots[r], sums_slots[0]
        )
        packed = sums[0:size, :]
        diagonal = sums[size : size + 1, :]
        turned = jnp.transpose(packed)
        on_diagonal = i_at == j_at
        identity = jnp.where(on_diagonal, 1.0, 0.0)
        gram = jnp.where(j_at > i_at, packed, jnp.where(on_diagonal, diagonal, turned))
        projected = jnp.where(j_at > i_at, turned, packed)
        residual = identity - gram
        right = chosen_ref[pl.ds(panel, 1), :]
        left = widen(chosen_col_ref[panel], size)
        spacing = right - left + identity
        update = jnp.where(
            on_diagonal, 0.5 * residual, (projected + right * residual) / spacing
        )
        v = identity + update
        gv = jnp.dot(gram, v, precision=HIGHEST, preferred_element_type=jnp.float32)
        column_sums = jnp.sum(v * gv, axis=0, keepdims=True)
        matrix_order = float(here * rows)
        v = v * jnp.sqrt(matrix_order / column_sums)
        v_full[...] = jnp.transpose(v)
        new_roots = (
            jnp.sum(jnp.where(on_diagonal, projected, 0.0), axis=0, keepdims=True) / diagonal
        )
        for c in range(cols):
            v_send[c, 0:width, :] = v_full[c * width : (c + 1) * width, :]
            v_send[c, width : width + 8, :] = jnp.broadcast_to(new_roots, (8, size))

        def send_update(step, carry):
            update_copy(step).start()
            return carry

        lax.fori_loop(1, total, send_update, 0)
        update_out[panel] = v_send[col]

    for c in range(cols):
        for k in range(own):
            from_row = k * spread + c % spread

            @pl.when(jnp.logical_or(row != from_row, col != c))
            def _():
                pltpu.make_async_remote_copy(
                    src_ref=v_send.at[0],
                    dst_ref=update_out.at[c * own + k],
                    send_sem=v_send_sem.at[0],
                    recv_sem=v_recv_sem.at[c * own + k],
                    device_id=(from_row, c),
                    device_id_type=MESH,
                ).wait_recv()

    @pl.when(owns)
    def _():
        def sent(step, carry):
            update_copy(step).wait_send()
            return carry

        lax.fori_loop(1, total, sent, 0)

    for k in range(own):

        @pl.when(owner_row(k) != row)
        def _():
            sums_copy(k).wait_send()

    @pl.when(row < rows - 1)
    def _():
        for copy in halo_copies:
            copy.wait_send()

    def written(panel, carry):
        out_copy(panel).wait()
        return carry

    lax.fori_loop(0, panels, written, 0)


def finish_kernel(width, v_ref, formed_ref, out_ref):
    high, low = split(v_ref[0, 0:width, :])
    parts = jnp.dot(
        jnp.concatenate([high, low], axis=0), formed_ref[0], preferred_element_type=jnp.float32
    )
    out_ref[0] = parts[0:width] + parts[width : 2 * width]


def pick_roots(secular_roots, column_order):
    panel_slots = jnp.arange(secular_roots.shape[1], dtype=jnp.int32)
    selector = (column_order[:, :, None] == panel_slots[None, None, :]).astype(jnp.float32)
    return jnp.sum(selector * secular_roots[:, None, :], axis=2)


def shards(
    pole_values,
    rank_one,
    deflated,
    onsite_energy,
    secular_roots,
    column_order,
    q_blocks,
    diag_blocks,
    coupling_blocks,
):
    rows, cols = lax.axis_size("row"), lax.axis_size("col")
    here = pole_values.shape[0]
    panels, size = secular_roots.shape
    block_count, block, _ = q_blocks.shape
    width = size // cols
    own = panels // cols
    total = rows * cols
    own_pad = -(-own // 8) * 8
    chosen = pick_roots(secular_roots, column_order)
    chosen_col = jnp.broadcast_to(chosen[:, :, None], (panels, size, LANES))
    vmem = pl.BlockSpec(memory_space=pltpu.VMEM)
    f32, bf16 = jnp.float32, jnp.bfloat16
    dma = pltpu.SemaphoreType.DMA
    formed, update = pl.pallas_call(
        functools.partial(merge_kernel, rows, cols),
        out_shape=(
            jax.ShapeDtypeStruct((panels, size, here), bf16),
            jax.ShapeDtypeStruct((panels, width + 8, size), f32),
        ),
        in_specs=[vmem] * 9,
        out_specs=(pl.BlockSpec(memory_space=pl.ANY), vmem),
        scratch_shapes=[
            pltpu.VMEM((16, here), f32),
            pltpu.VMEM((16, block), f32),
            pltpu.VMEM((block, block), bf16),
            pltpu.VMEM((own_pad, size), f32),
            pltpu.VMEM((total, own_pad, size), f32),
            pltpu.VMEM((panels, size, LANES), f32),
            pltpu.VMEM((block_count, 2, 2, block, block), bf16),
            pltpu.VMEM((panels, size, here), bf16),
            pltpu.VMEM((size, block), bf16),
            pltpu.VMEM((own, size + 8, size), f32),
            pltpu.VMEM((rows, size + 8, size), f32),
            pltpu.VMEM((size, size), f32),
            pltpu.VMEM((cols, width + 8, size), f32),
            dma((panels,)),
            dma((2,)),
            dma((2,)),
            dma((total,)),
            dma((total,)),
            dma((own,)),
            dma((rows,)),
            dma((total,)),
            dma((panels,)),
        ],
        compiler_params=pltpu.CompilerParams(
            collective_id=0, has_side_effects=True, vmem_limit_bytes=60 * 2**20
        ),
        name="merge",
    )(
        pole_values.reshape(1, here),
        rank_one.reshape(1, here),
        deflated.reshape(1, here),
        onsite_energy.reshape(1, here),
        chosen,
        chosen_col,
        q_blocks,
        diag_blocks,
        coupling_blocks,
    )
    refined = pl.pallas_call(
        functools.partial(finish_kernel, width),
        grid=(panels,),
        out_shape=jax.ShapeDtypeStruct((panels, width, here), f32),
        in_specs=[
            pl.BlockSpec((1, width + 8, size), lambda p: (p, 0, 0)),
            pl.BlockSpec((1, size, here), lambda p: (p, 0, 0)),
        ],
        out_specs=pl.BlockSpec((1, width, here), lambda p: (p, 0, 0)),
        compiler_params=pltpu.CompilerParams(vmem_limit_bytes=32 * 2**20),
        name="finish",
    )(update, formed)
    new_roots = lax.dynamic_slice_in_dim(
        update[:, width, :], lax.axis_index("col") * width, width, 1
    )
    return (jnp.swapaxes(refined, 1, 2), new_roots)


def solution(mesh):
    placed = (
        P("row"),
        P("row"),
        P("row"),
        P("row"),
        P(),
        P(),
        P("row", None, None),
        P("row", None, None),
        P("row", None, None),
    )
    return jax.shard_map(
        shards,
        mesh=mesh,
        in_specs=placed,
        out_specs=(P(None, "row", "col"), P(None, "col")),
        check_vma=False,
    )
```

```python
import functools

import jax
import jax.numpy as jnp
from jax import lax
from jax.experimental import pallas as pl
from jax.experimental.pallas import tpu as pltpu
from jax.sharding import PartitionSpec as P

EPSILON = 1e-06
HIGHEST = lax.Precision.HIGHEST
MESH = pl.DeviceIdType.MESH
LANES = 128


def dot_nt(a, b):
    return lax.dot_general(a, b, (((1,), (1,)), ((), ())), preferred_element_type=jnp.float32)


def split(x):
    high = x.astype(jnp.bfloat16)
    return high, (x - high.astype(jnp.float32)).astype(jnp.bfloat16)


def widen(x, width):
    return jnp.concatenate([x] * (width // x.shape[1]), axis=1)


def column_form(row):
    return jnp.transpose(jnp.broadcast_to(row, (LANES, row.shape[1])))


def merge_kernel(
    rows,
    cols,
    pole_ref,
    rank_ref,
    defl_ref,
    onsite_ref,
    roots_ref,
    order_ref,
    q_hbm,
    diag_hbm,
    coup_hbm,
    refined_hbm,
    roots_out,
    q_ref,
    diag_ref,
    coup_ref,
    chosen_col_ref,
    update_out,
    stage,
    pw,
    halo_pw,
    halo_q,
    sq_send,
    sq_slots,
    factor_col,
    hmat,
    formed,
    halo,
    sums_send,
    sums_slots,
    v_full,
    v_send,
    in_sem,
    out_sem,
    halo_send_sem,
    halo_recv_sem,
    sq_send_sem,
    sq_recv_sem,
    sums_send_sem,
    sums_recv_sem,
    v_send_sem,
    v_recv_sem,
):
    row = lax.axis_index("row")
    col = lax.axis_index("col")
    me = row * cols + col
    total = rows * cols
    panels, size = roots_ref.shape
    own = panels // cols
    block_count, block, _ = q_ref.shape
    here = block_count * block
    width = size // cols
    spread = rows // own

    in_copies = [
        pltpu.make_async_copy(source, target, in_sem.at[n])
        for n, (source, target) in enumerate(
            ((q_hbm, q_ref), (coup_hbm, coup_ref), (diag_hbm, diag_ref))
        )
    ]
    for copy in in_copies:
        copy.start()

    barrier = pltpu.get_barrier_semaphore()

    def greet(step, carry):
        other = lax.rem(me + step, total)
        pl.semaphore_signal(
            barrier, inc=1, device_id=(other // cols, lax.rem(other, cols)), device_id_type=MESH
        )
        return carry

    lax.fori_loop(1, total, greet, 0)

    weights = rank_ref[...] * (1 - defl_ref[...]).astype(jnp.float32)
    pw[0:8, :] = jnp.broadcast_to(pole_ref[...], (8, here))
    pw[8:16, :] = jnp.broadcast_to(weights, (8, here))

    i_at = lax.broadcasted_iota(jnp.int32, (size, size), 0)
    j_at = lax.broadcasted_iota(jnp.int32, (size, size), 1)

    def choose(panel, carry=0):
        order = column_form(order_ref[pl.ds(panel, 1), :].astype(jnp.float32))
        selector = jnp.where(widen(order, size) == j_at.astype(jnp.float32), 1.0, 0.0)
        selector = selector.astype(jnp.bfloat16)
        roots = column_form(roots_ref[pl.ds(panel, 1), :])
        high, low = split(roots)
        rest = (roots - high.astype(jnp.float32)) - low.astype(jnp.float32)
        picked = [
            jnp.dot(selector, part, preferred_element_type=jnp.float32)
            for part in (high, low, rest.astype(jnp.bfloat16))
        ]
        chosen_col_ref[panel] = (picked[0] + picked[1]) + picked[2]
        return carry

    def cauchy_of(poles, weight_row, panel):
        chosen = widen(chosen_col_ref[panel], poles.shape[1])
        return weight_row / (poles - chosen)

    sq_send[...] = jnp.zeros_like(sq_send)
    for k in range(own):
        choose(col * own + k)

        def add_squares(b, acc):
            lanes = pl.ds(pl.multiple_of(b * block, block), block)
            c = cauchy_of(pw[0:1, lanes], pw[8:9, lanes], col * own + k)
            c = c * c
            for t in range(block // LANES):
                acc = acc + c[:, t * LANES : (t + 1) * LANES]
            return acc

        acc = lax.fori_loop(0, block_count, add_squares, jnp.zeros((size, LANES), jnp.float32))
        sq_send[k : k + 1, :] = jnp.sum(jnp.transpose(acc), axis=0, keepdims=True)

    pl.semaphore_wait(barrier, total - 1)

    last = block_count - 1
    tail = pl.ds(here - block, block)
    halo_copies = [
        pltpu.make_async_remote_copy(
            src_ref=source,
            dst_ref=target,
            send_sem=halo_send_sem.at[n],
            recv_sem=halo_recv_sem.at[n],
            device_id=(lax.rem(row + 1, rows), col),
            device_id_type=MESH,
        )
        for n, (source, target) in enumerate(((q_hbm.at[last], halo_q), (pw.at[:, tail], halo_pw)))
    ]

    def square_copy(step):
        other = lax.rem(me + step, total)
        return pltpu.make_async_remote_copy(
            src_ref=sq_send,
            dst_ref=sq_slots.at[me],
            send_sem=sq_send_sem.at[step],
            recv_sem=sq_recv_sem.at[me],
            device_id=(other // cols, lax.rem(other, cols)),
            device_id_type=MESH,
        )

    def send_squares(step, carry):
        square_copy(step).start()
        return carry

    lax.fori_loop(1, total, send_squares, 0)

    @pl.when(row < rows - 1)
    def _():
        for copy in halo_copies:
            copy.start()

    sq_slots[me] = sq_send[...]

    lax.fori_loop(
        own, panels, lambda n, carry: choose(lax.rem(col * own + n, panels), carry), 0
    )
    for copy in in_copies:
        copy.wait()

    for b in range(block_count):
        hmat[b, 0] = coup_ref[b].astype(jnp.bfloat16)
        hmat[b, 1] = (0.5 * diag_ref[b]).astype(jnp.bfloat16)

    def await_squares(step, carry):
        other = lax.rem(me + step, total)
        square_copy(step).wait_send()
        pltpu.make_async_remote_copy(
            src_ref=sq_send,
            dst_ref=sq_slots.at[other],
            send_sem=sq_send_sem.at[step],
            recv_sem=sq_recv_sem.at[other],
            device_id=(other // cols, lax.rem(other, cols)),
            device_id_type=MESH,
        ).wait_recv()
        return carry

    lax.fori_loop(1, total, await_squares, 0)

    for c in range(cols):
        sums = lax.fori_loop(
            0, rows, lambda r, a: a + sq_slots[r * cols + c], jnp.zeros(sq_send.shape, jnp.float32)
        )
        factor = lax.rsqrt(sums + EPSILON)
        for k in range(own):
            factor_col[c * own + k] = column_form(factor[k : k + 1, :])

    def form_block(poles, weight_row, panel, q_block):
        scaled = cauchy_of(poles, weight_row, panel) * widen(factor_col[panel], block)
        return dot_nt(scaled.astype(jnp.bfloat16), q_block).astype(jnp.bfloat16)

    def form_panel(panel):
        for b in range(block_count):
            lanes = pl.ds(b * block, block)
            formed[panel, :, lanes] = form_block(pw[0:1, lanes], pw[8:9, lanes], panel, q_ref[b])

    def form_group(group):
        for b in range(block_count):
            lanes = pl.ds(b * block, block)
            scaled = [
                cauchy_of(pw[0:1, lanes], pw[8:9, lanes], group * own + k)
                * widen(factor_col[group * own + k], block)
                for k in range(own)
            ]
            scaled = jnp.concatenate([part.astype(jnp.bfloat16) for part in scaled], axis=0)
            result = dot_nt(scaled, q_ref[b]).astype(jnp.bfloat16)
            for k in range(own):
                formed[group * own + k, :, lanes] = result[k * size : (k + 1) * size]

    @pl.when(row > 0)
    def _():
        for copy in halo_copies:
            copy.wait_recv()

    def owner_row(k):
        return k * spread + lax.rem(col, spread)

    def sums_copy(k):
        return pltpu.make_async_remote_copy(
            src_ref=sums_send.at[k],
            dst_ref=sums_slots.at[row],
            send_sem=sums_send_sem.at[k],
            recv_sem=sums_recv_sem.at[row],
            device_id=(owner_row(k), col),
            device_id_type=MESH,
        )

    def own_panel(k, carry):
        panel = col * own + k
        form_panel(panel)

        @pl.when(row > 0)
        def _():
            halo[...] = form_block(halo_pw[0:1, :], halo_pw[8:9, :], panel, halo_q[...])

        @pl.when(row == 0)
        def _():
            halo[...] = jnp.zeros_like(halo)

        gram = jnp.zeros((size, size), jnp.float32)
        half = jnp.zeros((size, size), jnp.float32)
        for b in range(block_count):
            lanes = pl.ds(b * block, block)
            now = formed[panel, :, lanes]
            before = halo[...] if b == 0 else formed[panel, :, pl.ds((b - 1) * block, block)]
            image = dot_nt(before, hmat[b, 0]) + dot_nt(now, hmat[b, 1])
            image = image + 0.5 * onsite_ref[0:1, lanes] * now.astype(jnp.float32)
            high, low = split(image)
            gram = gram + dot_nt(now, now)
            half = half + dot_nt(now, high) + dot_nt(now, low)
        projected = half + jnp.transpose(half)
        sums_send[k, 0:size, :] = jnp.where(j_at > i_at, gram, projected)
        diagonal = jnp.sum(jnp.where(i_at == j_at, gram, 0.0), axis=0, keepdims=True)
        sums_send[k, size : size + 8, :] = jnp.broadcast_to(diagonal, (8, size))

        @pl.when(owner_row(k) != row)
        def _():
            sums_copy(k).start()

        @pl.when(owner_row(k) == row)
        def _():
            sums_slots[row] = sums_send[k]

        return carry

    lax.fori_loop(0, own, own_panel, 0)

    def form_rest(n, carry):
        form_group(lax.rem(col + n, cols))
        return carry

    late = max(1, cols - 1)
    lax.fori_loop(1, late, form_rest, 0)

    mine = row // spread
    owns = owner_row(mine) == row

    def update_copy(step):
        other = lax.rem(me + step, total)
        other_col = lax.rem(other, cols)
        return pltpu.make_async_remote_copy(
            src_ref=v_send.at[other_col],
            dst_ref=update_out.at[col * own + mine],
            send_sem=v_send_sem.at[step],
            recv_sem=v_recv_sem.at[col * own + mine],
            device_id=(other // cols, other_col),
            device_id_type=MESH,
        )

    @pl.when(owns)
    def _():
        panel = col * own + mine

        def arrive(step, carry):
            other = lax.rem(row + step, rows)
            pltpu.make_async_remote_copy(
                src_ref=sums_send.at[0],
                dst_ref=sums_slots.at[other],
                send_sem=sums_send_sem.at[0],
                recv_sem=sums_recv_sem.at[other],
                device_id=(other, col),
                device_id_type=MESH,
            ).wait_recv()
            return carry

        lax.fori_loop(1, rows, arrive, 0)
        sums = lax.fori_loop(
            1, rows, lambda r, a: a + sums_slots[r], sums_slots[0]
        )
        packed = sums[0:size, :]
        diagonal = sums[size : size + 1, :]
        turned = jnp.transpose(packed)
        on_diagonal = i_at == j_at
        identity = jnp.where(on_diagonal, 1.0, 0.0)
        gram = jnp.where(j_at > i_at, packed, jnp.where(on_diagonal, diagonal, turned))
        projected = jnp.where(j_at > i_at, turned, packed)
        residual = identity - gram
        right = jnp.transpose(chosen_col_ref[panel])[0:1, :]
        left = widen(chosen_col_ref[panel], size)
        spacing = right - left + identity
        update = jnp.where(
            on_diagonal, 0.5 * residual, (projected + right * residual) / spacing
        )
        v = identity + update
        gv = jnp.dot(gram, v, precision=HIGHEST, preferred_element_type=jnp.float32)
        column_sums = jnp.sum(v * gv, axis=0, keepdims=True)
        matrix_order = float(here * rows)
        v = v * jnp.sqrt(matrix_order / column_sums)
        v_full[...] = jnp.transpose(v)
        new_roots = (
            jnp.sum(jnp.where(on_diagonal, projected, 0.0), axis=0, keepdims=True) / diagonal
        )
        for c in range(cols):
            v_send[c, 0:width, :] = v_full[c * width : (c + 1) * width, :]
            v_send[c, width : width + 8, :] = jnp.broadcast_to(new_roots, (8, size))

        def send_update(step, carry):
            update_copy(step).start()
            return carry

        lax.fori_loop(1, total, send_update, 0)
        update_out[panel] = v_send[col]

    lax.fori_loop(late, cols, form_rest, 0)

    def out_copy(n):
        panel = lax.rem(n, cols) * own + n // cols
        return pltpu.make_async_copy(
            stage.at[lax.rem(n, own)], refined_hbm.at[panel], out_sem.at[lax.rem(n, own)]
        )

    def finish(n, carry):
        c, k = lax.rem(n, cols), n // cols
        panel = c * own + k
        from_row = k * spread + lax.rem(c, spread)

        @pl.when(jnp.logical_or(row != from_row, col != c))
        def _():
            pltpu.make_async_remote_copy(
                src_ref=v_send.at[0],
                dst_ref=update_out.at[panel],
                send_sem=v_send_sem.at[0],
                recv_sem=v_recv_sem.at[panel],
                device_id=(from_row, c),
                device_id_type=MESH,
            ).wait_recv()

        high, low = split(update_out[panel, 0:width, :])
        parts = jnp.dot(
            jnp.concatenate([high, low], axis=0),
            formed[panel],
            preferred_element_type=jnp.float32,
        )
        roots_out[panel] = update_out[panel, width : width + 8, :]

        @pl.when(n >= own)
        def _():
            out_copy(n - own).wait()

        stage[lax.rem(n, own)] = parts[0:width] + parts[width : 2 * width]
        out_copy(n).start()
        return carry

    lax.fori_loop(0, panels, finish, 0)

    @pl.when(owns)
    def _():
        def sent(step, carry):
            update_copy(step).wait_send()
            return carry

        lax.fori_loop(1, total, sent, 0)

    for k in range(own):

        @pl.when(owner_row(k) != row)
        def _():
            sums_copy(k).wait_send()

    @pl.when(row < rows - 1)
    def _():
        for copy in halo_copies:
            copy.wait_send()

    def written(n, carry):
        out_copy(n).wait()
        return carry

    lax.fori_loop(panels - own, panels, written, 0)


def shards(
    pole_values,
    rank_one,
    deflated,
    onsite_energy,
    secular_roots,
    column_order,
    q_blocks,
    diag_blocks,
    coupling_blocks,
):
    rows, cols = lax.axis_size("row"), lax.axis_size("col")
    here = pole_values.shape[0]
    panels, size = secular_roots.shape
    block_count, block, _ = q_blocks.shape
    width = size // cols
    own = panels // cols
    total = rows * cols
    own_pad = -(-own // 8) * 8
    vmem = pl.BlockSpec(memory_space=pltpu.VMEM)
    f32, bf16 = jnp.float32, jnp.bfloat16
    dma = pltpu.SemaphoreType.DMA
    anywhere = pl.BlockSpec(memory_space=pl.ANY)
    refined, new_roots = pl.pallas_call(
        functools.partial(merge_kernel, rows, cols),
        out_shape=(
            jax.ShapeDtypeStruct((panels, width, here), f32),
            jax.ShapeDtypeStruct((panels, 8, size), f32),
        ),
        in_specs=[vmem] * 6 + [anywhere] * 3,
        out_specs=(anywhere, vmem),
        scratch_shapes=[
            pltpu.VMEM(q_blocks.shape, bf16),
            pltpu.VMEM(diag_blocks.shape, f32),
            pltpu.VMEM(coupling_blocks.shape, f32),
            pltpu.VMEM((panels, size, LANES), f32),
            pltpu.VMEM((panels, width + 8, size), f32),
            pltpu.VMEM((own, width, here), f32),
            pltpu.VMEM((16, here), f32),
            pltpu.VMEM((16, block), f32),
            pltpu.VMEM((block, block), bf16),
            pltpu.VMEM((own_pad, size), f32),
            pltpu.VMEM((total, own_pad, size), f32),
            pltpu.VMEM((panels, size, LANES), f32),
            pltpu.VMEM((block_count, 2, block, block), bf16),
            pltpu.VMEM((panels, size, here), bf16),
            pltpu.VMEM((size, block), bf16),
            pltpu.VMEM((own, size + 8, size), f32),
            pltpu.VMEM((rows, size + 8, size), f32),
            pltpu.VMEM((size, size), f32),
            pltpu.VMEM((cols, width + 8, size), f32),
            dma((3,)),
            dma((own,)),
            dma((2,)),
            dma((2,)),
            dma((total,)),
            dma((total,)),
            dma((own,)),
            dma((rows,)),
            dma((total,)),
            dma((panels,)),
        ],
        compiler_params=pltpu.CompilerParams(
            collective_id=0, has_side_effects=True, vmem_limit_bytes=60 * 2**20
        ),
        name="merge",
    )(
        pole_values.reshape(1, here),
        rank_one.reshape(1, here),
        deflated.reshape(1, here),
        onsite_energy.reshape(1, here),
        secular_roots,
        column_order,
        q_blocks,
        diag_blocks,
        coupling_blocks,
    )
    new_roots = lax.dynamic_slice_in_dim(
        new_roots[:, 0, :], lax.axis_index("col") * width, width, 1
    )
    return (jnp.swapaxes(refined, 1, 2), new_roots)


def solution(mesh):
    placed = (
        P("row"),
        P("row"),
        P("row"),
        P("row"),
        P(),
        P(),
        P("row", None, None),
        P("row", None, None),
        P("row", None, None),
    )
    return jax.shard_map(
        shards,
        mesh=mesh,
        in_specs=placed,
        out_specs=(P(None, "row", "col"), P(None, "col")),
        check_vma=False,
    )
```

```python
import functools

import jax
import jax.numpy as jnp
from jax import lax
from jax.experimental import pallas as pl
from jax.experimental.pallas import tpu as pltpu
from jax.sharding import PartitionSpec as P

EPSILON = 1e-06
HIGHEST = lax.Precision.HIGHEST
MESH = pl.DeviceIdType.MESH
LANES = 128


def dot_nt(a, b):
    return lax.dot_general(a, b, (((1,), (1,)), ((), ())), preferred_element_type=jnp.float32)


def split(x):
    high = x.astype(jnp.bfloat16)
    return high, (x - high.astype(jnp.float32)).astype(jnp.bfloat16)


def widen(x, width):
    return jnp.concatenate([x] * (width // x.shape[1]), axis=1)


def column_form(row):
    return jnp.transpose(jnp.broadcast_to(row, (LANES, row.shape[1])))


def merge_kernel(
    rows,
    cols,
    pole_ref,
    rank_ref,
    defl_ref,
    onsite_ref,
    roots_ref,
    order_ref,
    q_hbm,
    diag_hbm,
    coup_hbm,
    refined_hbm,
    roots_out,
    q_ref,
    diag_ref,
    coup_ref,
    chosen_col_ref,
    update_out,
    stage,
    pw,
    halo_pw,
    halo_q,
    sq_send,
    sq_slots,
    factor_col,
    hmat,
    formed,
    halo,
    sums_send,
    plane_slots,
    sums_slots,
    v_full,
    relay,
    in_sem,
    out_sem,
    halo_send_sem,
    halo_recv_sem,
    sq_send_sem,
    sq_recv_sem,
    plane_send_sem,
    plane_recv_sem,
    sums_send_sem,
    sums_recv_sem,
    relay_send_sem,
    relay_recv_sem,
    v_send_sem,
    v_recv_sem,
):
    row = lax.axis_index("row")
    col = lax.axis_index("col")
    me = row * cols + col
    total = rows * cols
    panels, size = roots_ref.shape
    own = panels // cols
    block_count, block, _ = q_ref.shape
    here = block_count * block
    width = size // cols
    spread = rows // own
    sub = size // LANES
    high_row, low_row = row // spread, lax.rem(row, spread)
    collects = low_row == lax.rem(col, spread)
    collector = high_row * spread + lax.rem(col, spread)

    in_copies = [
        pltpu.make_async_copy(source, target, in_sem.at[n])
        for n, (source, target) in enumerate(
            ((q_hbm, q_ref), (coup_hbm, coup_ref), (diag_hbm, diag_ref))
        )
    ]
    for copy in in_copies:
        copy.start()

    barrier = pltpu.get_barrier_semaphore()

    def greet(step, carry):
        other = lax.rem(me + step, total)
        pl.semaphore_signal(
            barrier, inc=1, device_id=(other // cols, lax.rem(other, cols)), device_id_type=MESH
        )
        return carry

    lax.fori_loop(1, total, greet, 0)

    weights = rank_ref[...] * (1 - defl_ref[...]).astype(jnp.float32)
    pw[0:8, :] = jnp.broadcast_to(pole_ref[...], (8, here))
    pw[8:16, :] = jnp.broadcast_to(weights, (8, here))

    i_at = lax.broadcasted_iota(jnp.int32, (size, size), 0)
    j_at = lax.broadcasted_iota(jnp.int32, (size, size), 1)

    def choose(panel, carry=0):
        order = column_form(order_ref[pl.ds(panel, 1), :].astype(jnp.float32))
        selector = jnp.where(widen(order, size) == j_at.astype(jnp.float32), 1.0, 0.0)
        selector = selector.astype(jnp.bfloat16)
        roots = column_form(roots_ref[pl.ds(panel, 1), :])
        high, low = split(roots)
        rest = (roots - high.astype(jnp.float32)) - low.astype(jnp.float32)
        picked = [
            jnp.dot(selector, part, preferred_element_type=jnp.float32)
            for part in (high, low, rest.astype(jnp.bfloat16))
        ]
        chosen_col_ref[panel] = (picked[0] + picked[1]) + picked[2]
        return carry

    def cauchy_of(poles, weight_row, panel):
        chosen = widen(chosen_col_ref[panel], poles.shape[1])
        return weight_row / (poles - chosen)

    sq_send[...] = jnp.zeros_like(sq_send)
    for k in range(own):
        choose(col * own + k)

        def add_squares(b, acc):
            lanes = pl.ds(pl.multiple_of(b * block, block), block)
            c = cauchy_of(pw[0:1, lanes], pw[8:9, lanes], col * own + k)
            c = c * c
            for t in range(block // LANES):
                acc = acc + c[:, t * LANES : (t + 1) * LANES]
            return acc

        acc = lax.fori_loop(0, block_count, add_squares, jnp.zeros((size, LANES), jnp.float32))
        squares = jnp.sum(jnp.transpose(acc), axis=0, keepdims=True)
        for t in range(sub):
            sq_send[k * sub + t : k * sub + t + 1, :] = squares[:, t * LANES : (t + 1) * LANES]

    pl.semaphore_wait(barrier, total - 1)

    last = block_count - 1
    tail = pl.ds(here - block, block)
    halo_copies = [
        pltpu.make_async_remote_copy(
            src_ref=source,
            dst_ref=target,
            send_sem=halo_send_sem.at[n],
            recv_sem=halo_recv_sem.at[n],
            device_id=(lax.rem(row + 1, rows), col),
            device_id_type=MESH,
        )
        for n, (source, target) in enumerate(((q_hbm.at[last], halo_q), (pw.at[:, tail], halo_pw)))
    ]

    def square_copy(step):
        other = lax.rem(me + step, total)
        return pltpu.make_async_remote_copy(
            src_ref=sq_send,
            dst_ref=sq_slots.at[me],
            send_sem=sq_send_sem.at[step],
            recv_sem=sq_recv_sem.at[me],
            device_id=(other // cols, lax.rem(other, cols)),
            device_id_type=MESH,
        )

    def send_squares(step, carry):
        square_copy(step).start()
        return carry

    lax.fori_loop(1, total, send_squares, 0)

    @pl.when(row < rows - 1)
    def _():
        for copy in halo_copies:
            copy.start()

    sq_slots[me] = sq_send[...]

    lax.fori_loop(
        own, panels, lambda n, carry: choose(lax.rem(col * own + n, panels), carry), 0
    )
    for copy in in_copies:
        copy.wait()

    for b in range(block_count):
        hmat[b, 0] = coup_ref[b].astype(jnp.bfloat16)
        hmat[b, 1] = (0.5 * diag_ref[b]).astype(jnp.bfloat16)

    def await_squares(step, carry):
        other = lax.rem(me + step, total)
        square_copy(step).wait_send()
        pltpu.make_async_remote_copy(
            src_ref=sq_send,
            dst_ref=sq_slots.at[other],
            send_sem=sq_send_sem.at[step],
            recv_sem=sq_recv_sem.at[other],
            device_id=(other // cols, lax.rem(other, cols)),
            device_id_type=MESH,
        ).wait_recv()
        return carry

    lax.fori_loop(1, total, await_squares, 0)

    for c in range(cols):
        sums = lax.fori_loop(
            0, rows, lambda r, a: a + sq_slots[r * cols + c], jnp.zeros(sq_send.shape, jnp.float32)
        )
        factor = lax.rsqrt(sums + EPSILON)
        for k in range(own):
            factor_col[c * own + k] = column_form(
                jnp.concatenate(
                    [factor[k * sub + t : k * sub + t + 1, :] for t in range(sub)], axis=1
                )
            )

    def form_block(poles, weight_row, panel, q_block):
        scaled = cauchy_of(poles, weight_row, panel) * widen(factor_col[panel], block)
        return dot_nt(scaled.astype(jnp.bfloat16), q_block).astype(jnp.bfloat16)

    def form_panel(panel):
        for b in range(block_count):
            lanes = pl.ds(b * block, block)
            formed[panel, :, lanes] = form_block(pw[0:1, lanes], pw[8:9, lanes], panel, q_ref[b])

    def form_group(group):
        for b in range(block_count):
            lanes = pl.ds(b * block, block)
            scaled = [
                cauchy_of(pw[0:1, lanes], pw[8:9, lanes], group * own + k)
                * widen(factor_col[group * own + k], block)
                for k in range(own)
            ]
            scaled = jnp.concatenate([part.astype(jnp.bfloat16) for part in scaled], axis=0)
            result = dot_nt(scaled, q_ref[b]).astype(jnp.bfloat16)
            for k in range(own):
                formed[group * own + k, :, lanes] = result[k * size : (k + 1) * size]

    @pl.when(row > 0)
    def _():
        for copy in halo_copies:
            copy.wait_recv()

    def plane_copy(k, source_low):
        return pltpu.make_async_remote_copy(
            src_ref=sums_send.at[k],
            dst_ref=plane_slots.at[k, source_low],
            send_sem=plane_send_sem.at[k],
            recv_sem=plane_recv_sem.at[k, source_low],
            device_id=(collector, col),
            device_id_type=MESH,
        )

    def sums_copy(k, source_high):
        return pltpu.make_async_remote_copy(
            src_ref=sums_send.at[k],
            dst_ref=sums_slots.at[source_high],
            send_sem=sums_send_sem.at[k],
            recv_sem=sums_recv_sem.at[source_high],
            device_id=(k * spread + low_row, col),
            device_id_type=MESH,
        )

    def collect(k):
        def add(step, carry):
            other = lax.rem(low_row + step, spread)
            plane_copy(k, other).wait_recv()
            sums_send[k] += plane_slots[k, other]
            return carry

        lax.fori_loop(1, spread, add, 0)

        @pl.when(high_row != k)
        def _():
            sums_copy(k, high_row).start()

    def own_panel(k, carry):
        panel = col * own + k
        form_panel(panel)

        @pl.when(row > 0)
        def _():
            halo[...] = form_block(halo_pw[0:1, :], halo_pw[8:9, :], panel, halo_q[...])

        @pl.when(row == 0)
        def _():
            halo[...] = jnp.zeros_like(halo)

        gram = jnp.zeros((size, size), jnp.float32)
        half = jnp.zeros((size, size), jnp.float32)
        for b in range(block_count):
            lanes = pl.ds(b * block, block)
            now = formed[panel, :, lanes]
            before = halo[...] if b == 0 else formed[panel, :, pl.ds((b - 1) * block, block)]
            image = dot_nt(before, hmat[b, 0]) + dot_nt(now, hmat[b, 1])
            image = image + 0.5 * onsite_ref[0:1, lanes] * now.astype(jnp.float32)
            high, low = split(image)
            gram = gram + dot_nt(now, now)
            half = half + dot_nt(now, high) + dot_nt(now, low)
        projected = half + jnp.transpose(half)
        sums_send[k, 0:size, :] = jnp.where(j_at > i_at, gram, projected)
        diagonal = jnp.sum(jnp.where(i_at == j_at, gram, 0.0), axis=0, keepdims=True)
        sums_send[k, size : size + 8, :] = jnp.broadcast_to(diagonal, (8, size))

        @pl.when(jnp.logical_not(collects))
        def _():
            plane_copy(k, low_row).start()

        @pl.when(jnp.logical_and(collects, k > 0))
        def _():
            collect(k - 1)

        return carry

    lax.fori_loop(0, own, own_panel, 0)

    @pl.when(collects)
    def _():
        collect(own - 1)

    def form_rest(n, carry):
        form_group(lax.rem(col + n, cols))
        return carry

    late = max(1, cols - 1)
    lax.fori_loop(1, late, form_rest, 0)

    def relay_copy(step):
        other = lax.rem(high_row + step, own)
        return pltpu.make_async_remote_copy(
            src_ref=relay.at[high_row],
            dst_ref=relay.at[high_row],
            send_sem=relay_send_sem.at[step],
            recv_sem=relay_recv_sem.at[high_row],
            device_id=(other * spread + low_row, col),
            device_id_type=MESH,
        )

    def update_copy(k, step):
        other = lax.rem(low_row * cols + col + step, spread * cols)
        other_col = lax.rem(other, cols)
        return pltpu.make_async_remote_copy(
            src_ref=relay.at[k, other_col],
            dst_ref=update_out.at[col * own + k],
            send_sem=v_send_sem.at[k, step],
            recv_sem=v_recv_sem.at[col * own + k],
            device_id=(high_row * spread + other // cols, other_col),
            device_id_type=MESH,
        )

    def forward(k):
        def send_update(step, carry):
            update_copy(k, step).start()
            return carry

        lax.fori_loop(1, spread * cols, send_update, 0)
        update_out[col * own + k] = relay[k, col]

    @pl.when(collects)
    def _():
        panel = col * own + high_row

        def arrive(step, total_sums):
            other = lax.rem(high_row + step, own)
            sums_copy(high_row, other).wait_recv()
            return total_sums + sums_slots[other]

        sums = lax.fori_loop(1, own, arrive, sums_send[high_row])
        packed = sums[0:size, :]
        diagonal = sums[size : size + 1, :]
        turned = jnp.transpose(packed)
        on_diagonal = i_at == j_at
        identity = jnp.where(on_diagonal, 1.0, 0.0)
        gram = jnp.where(j_at > i_at, packed, jnp.where(on_diagonal, diagonal, turned))
        projected = jnp.where(j_at > i_at, turned, packed)
        residual = identity - gram
        right = jnp.transpose(chosen_col_ref[panel])[0:1, :]
        left = widen(chosen_col_ref[panel], size)
        spacing = right - left + identity
        update = jnp.where(
            on_diagonal, 0.5 * residual, (projected + right * residual) / spacing
        )
        v = identity + update
        gv = jnp.dot(gram, v, precision=HIGHEST, preferred_element_type=jnp.float32)
        column_sums = jnp.sum(v * gv, axis=0, keepdims=True)
        matrix_order = float(here * rows)
        v = v * jnp.sqrt(matrix_order / column_sums)
        v_full[...] = jnp.transpose(v)
        new_roots = (
            jnp.sum(jnp.where(on_diagonal, projected, 0.0), axis=0, keepdims=True) / diagonal
        )
        for c in range(cols):
            lanes = slice(c * width, (c + 1) * width)
            relay[high_row, c, 0:width, :] = v_full[lanes, :]
            relay[high_row, c, width : width + 8, 0:width] = jnp.broadcast_to(
                new_roots[:, lanes], (8, width)
            )
        for step in range(1, own):
            relay_copy(step).start()
        forward(high_row)

    lax.fori_loop(late, cols, form_rest, 0)

    @pl.when(collects)
    def _():
        def pass_on(step, carry):
            k = lax.rem(high_row + step, own)
            pltpu.make_async_remote_copy(
                src_ref=relay.at[k],
                dst_ref=relay.at[k],
                send_sem=relay_send_sem.at[step],
                recv_sem=relay_recv_sem.at[k],
                device_id=(k * spread + low_row, col),
                device_id_type=MESH,
            ).wait_recv()
            forward(k)
            return carry

        lax.fori_loop(1, own, pass_on, 0)

    def out_copy(n):
        panel = lax.rem(n, cols) * own + lax.rem(high_row + n // cols, own)
        return pltpu.make_async_copy(
            stage.at[lax.rem(n, own)], refined_hbm.at[panel], out_sem.at[lax.rem(n, own)]
        )

    def finish(n, carry):
        c, k = lax.rem(n, cols), lax.rem(high_row + n // cols, own)
        panel = c * own + k
        from_row = high_row * spread + lax.rem(c, spread)

        @pl.when(jnp.logical_or(row != from_row, col != c))
        def _():
            pltpu.make_async_remote_copy(
                src_ref=relay.at[0, 0],
                dst_ref=update_out.at[panel],
                send_sem=v_send_sem.at[0, 0],
                recv_sem=v_recv_sem.at[panel],
                device_id=(from_row, c),
                device_id_type=MESH,
            ).wait_recv()

        high, low = split(update_out[panel, 0:width, :])
        parts = jnp.dot(
            jnp.concatenate([high, low], axis=0),
            formed[panel],
            preferred_element_type=jnp.float32,
        )
        roots_out[pl.ds(panel, 1), :] = update_out[panel, width : width + 1, 0:width]

        @pl.when(n >= own)
        def _():
            out_copy(n - own).wait()

        stage[lax.rem(n, own)] = parts[0:width] + parts[width : 2 * width]
        out_copy(n).start()
        return carry

    lax.fori_loop(0, panels, finish, 0)

    @pl.when(collects)
    def _():
        def sent(n, carry):
            update_copy(n // (spread * cols - 1), 1 + lax.rem(n, spread * cols - 1)).wait_send()
            return carry

        lax.fori_loop(0, own * (spread * cols - 1), sent, 0)
        for step in range(1, own):
            relay_copy(step).wait_send()
        for k in range(own):

            @pl.when(high_row != k)
            def _():
                sums_copy(k, high_row).wait_send()

    @pl.when(jnp.logical_not(collects))
    def _():
        for k in range(own):
            plane_copy(k, low_row).wait_send()

    @pl.when(row < rows - 1)
    def _():
        for copy in halo_copies:
            copy.wait_send()

    def written(n, carry):
        out_copy(n).wait()
        return carry

    lax.fori_loop(panels - own, panels, written, 0)


def shards(
    pole_values,
    rank_one,
    deflated,
    onsite_energy,
    secular_roots,
    column_order,
    q_blocks,
    diag_blocks,
    coupling_blocks,
):
    rows, cols = lax.axis_size("row"), lax.axis_size("col")
    here = pole_values.shape[0]
    panels, size = secular_roots.shape
    block_count, block, _ = q_blocks.shape
    width = size // cols
    own = panels // cols
    total = rows * cols
    spread = rows // own
    sub = size // LANES
    squares_pad = -(-own * sub // 8) * 8
    vmem = pl.BlockSpec(memory_space=pltpu.VMEM)
    f32, bf16 = jnp.float32, jnp.bfloat16
    dma = pltpu.SemaphoreType.DMA
    anywhere = pl.BlockSpec(memory_space=pl.ANY)
    refined, new_roots = pl.pallas_call(
        functools.partial(merge_kernel, rows, cols),
        out_shape=(
            jax.ShapeDtypeStruct((panels, width, here), f32),
            jax.ShapeDtypeStruct((panels, width), f32),
        ),
        in_specs=[vmem] * 6 + [anywhere] * 3,
        out_specs=(anywhere, vmem),
        scratch_shapes=[
            pltpu.VMEM(q_blocks.shape, bf16),
            pltpu.VMEM(diag_blocks.shape, f32),
            pltpu.VMEM(coupling_blocks.shape, f32),
            pltpu.VMEM((panels, size, LANES), f32),
            pltpu.VMEM((panels, width + 8, size), f32),
            pltpu.VMEM((own, width, here), f32),
            pltpu.VMEM((16, here), f32),
            pltpu.VMEM((16, block), f32),
            pltpu.VMEM((block, block), bf16),
            pltpu.VMEM((squares_pad, LANES), f32),
            pltpu.VMEM((total, squares_pad, LANES), f32),
            pltpu.VMEM((panels, size, LANES), f32),
            pltpu.VMEM((block_count, 2, block, block), bf16),
            pltpu.VMEM((panels, size, here), bf16),
            pltpu.VMEM((size, block), bf16),
            pltpu.VMEM((own, size + 8, size), f32),
            pltpu.VMEM((own, spread, size + 8, size), f32),
            pltpu.VMEM((own, size + 8, size), f32),
            pltpu.VMEM((size, size), f32),
            pltpu.VMEM((own, cols, width + 8, size), f32),
            dma((3,)),
            dma((own,)),
            dma((2,)),
            dma((2,)),
            dma((total,)),
            dma((total,)),
            dma((own,)),
            dma((own, spread)),
            dma((own,)),
            dma((own,)),
            dma((own,)),
            dma((own,)),
            dma((own, spread * cols)),
            dma((panels,)),
        ],
        compiler_params=pltpu.CompilerParams(
            collective_id=0, has_side_effects=True, vmem_limit_bytes=60 * 2**20
        ),
        name="merge",
    )(
        pole_values.reshape(1, here),
        rank_one.reshape(1, here),
        deflated.reshape(1, here),
        onsite_energy.reshape(1, here),
        secular_roots,
        column_order,
        q_blocks,
        diag_blocks,
        coupling_blocks,
    )
    return (jnp.swapaxes(refined, 1, 2), new_roots)


def solution(mesh):
    placed = (
        P("row"),
        P("row"),
        P("row"),
        P("row"),
        P(),
        P(),
        P("row", None, None),
        P("row", None, None),
        P("row", None, None),
    )
    return jax.shard_map(
        shards,
        mesh=mesh,
        in_specs=placed,
        out_specs=(P(None, "row", "col"), P(None, "col")),
        check_vma=False,
    )
```

```python
import functools

import jax
import jax.numpy as jnp
from jax import lax
from jax.experimental import pallas as pl
from jax.experimental.pallas import tpu as pltpu
from jax.sharding import PartitionSpec as P

EPSILON = 1e-06
HIGHEST = lax.Precision.HIGHEST
MESH = pl.DeviceIdType.MESH
LANES = 128


def dot_nt(a, b):
    return lax.dot_general(a, b, (((1,), (1,)), ((), ())), preferred_element_type=jnp.float32)


def split(x):
    high = x.astype(jnp.bfloat16)
    return high, (x - high.astype(jnp.float32)).astype(jnp.bfloat16)


def widen(x, width):
    return jnp.concatenate([x] * (width // x.shape[1]), axis=1)


def column_form(row):
    return jnp.transpose(jnp.broadcast_to(row, (LANES, row.shape[1])))


def merge_kernel(
    rows,
    cols,
    pole_ref,
    rank_ref,
    defl_ref,
    onsite_ref,
    roots_ref,
    order_ref,
    q_hbm,
    diag_hbm,
    coup_hbm,
    refined_hbm,
    roots_out,
    q_ref,
    diag_ref,
    coup_ref,
    chosen_col_ref,
    update_out,
    stage,
    pw,
    halo_pw,
    halo_q,
    sq_send,
    sq_slots,
    factor_col,
    hmat,
    onsite_col,
    formed,
    halo,
    sums_send,
    plane_slots,
    sums_slots,
    v_full,
    relay,
    in_sem,
    out_sem,
    halo_send_sem,
    halo_recv_sem,
    sq_send_sem,
    sq_recv_sem,
    plane_send_sem,
    plane_recv_sem,
    sums_send_sem,
    sums_recv_sem,
    relay_send_sem,
    relay_recv_sem,
    v_send_sem,
    v_recv_sem,
):
    row = lax.axis_index("row")
    col = lax.axis_index("col")
    me = row * cols + col
    total = rows * cols
    panels, size = roots_ref.shape
    own = panels // cols
    block_count, block, _ = q_ref.shape
    here = block_count * block
    width = size // cols
    spread = rows // own
    sub = size // LANES
    high_row, low_row = row // spread, lax.rem(row, spread)
    collects = low_row == lax.rem(col, spread)
    collector = high_row * spread + lax.rem(col, spread)

    in_copies = [
        pltpu.make_async_copy(source, target, in_sem.at[n])
        for n, (source, target) in enumerate(
            ((q_hbm, q_ref), (coup_hbm, coup_ref), (diag_hbm, diag_ref))
        )
    ]
    for copy in in_copies:
        copy.start()

    barrier = pltpu.get_barrier_semaphore()

    def greet(step, carry):
        other = lax.rem(me + step, total)
        pl.semaphore_signal(
            barrier, inc=1, device_id=(other // cols, lax.rem(other, cols)), device_id_type=MESH
        )
        return carry

    lax.fori_loop(1, total, greet, 0)

    weights = rank_ref[...] * (1 - defl_ref[...]).astype(jnp.float32)
    pw[0:8, :] = jnp.broadcast_to(pole_ref[...], (8, here))
    pw[8:16, :] = jnp.broadcast_to(weights, (8, here))

    i_at = lax.broadcasted_iota(jnp.int32, (size, size), 0)
    j_at = lax.broadcasted_iota(jnp.int32, (size, size), 1)

    def choose(panel, carry=0):
        order = column_form(order_ref[pl.ds(panel, 1), :].astype(jnp.float32))
        selector = jnp.where(widen(order, size) == j_at.astype(jnp.float32), 1.0, 0.0)
        selector = selector.astype(jnp.bfloat16)
        roots = column_form(roots_ref[pl.ds(panel, 1), :])
        high, low = split(roots)
        rest = (roots - high.astype(jnp.float32)) - low.astype(jnp.float32)
        picked = [
            jnp.dot(selector, part, preferred_element_type=jnp.float32)
            for part in (high, low, rest.astype(jnp.bfloat16))
        ]
        chosen_col_ref[panel] = (picked[0] + picked[1]) + picked[2]
        return carry

    def cauchy_of(poles, weight_row, panel):
        chosen = widen(chosen_col_ref[panel], poles.shape[1])
        return weight_row / (poles - chosen)

    sq_send[...] = jnp.zeros_like(sq_send)
    for k in range(own):
        choose(col * own + k)

        def add_squares(b, acc):
            lanes = pl.ds(pl.multiple_of(b * block, block), block)
            c = cauchy_of(pw[0:1, lanes], pw[8:9, lanes], col * own + k)
            c = c * c
            for t in range(block // LANES):
                acc = acc + c[:, t * LANES : (t + 1) * LANES]
            return acc

        acc = lax.fori_loop(0, block_count, add_squares, jnp.zeros((size, LANES), jnp.float32))
        squares = jnp.sum(jnp.transpose(acc), axis=0, keepdims=True)
        for t in range(sub):
            sq_send[k * sub + t : k * sub + t + 1, :] = squares[:, t * LANES : (t + 1) * LANES]

    pl.semaphore_wait(barrier, total - 1)

    last = block_count - 1
    tail = pl.ds(here - block, block)
    halo_copies = [
        pltpu.make_async_remote_copy(
            src_ref=source,
            dst_ref=target,
            send_sem=halo_send_sem.at[n],
            recv_sem=halo_recv_sem.at[n],
            device_id=(lax.rem(row + 1, rows), col),
            device_id_type=MESH,
        )
        for n, (source, target) in enumerate(((q_hbm.at[last], halo_q), (pw.at[:, tail], halo_pw)))
    ]

    def square_copy(step):
        other = lax.rem(me + step, total)
        return pltpu.make_async_remote_copy(
            src_ref=sq_send,
            dst_ref=sq_slots.at[me],
            send_sem=sq_send_sem.at[step],
            recv_sem=sq_recv_sem.at[me],
            device_id=(other // cols, lax.rem(other, cols)),
            device_id_type=MESH,
        )

    def send_squares(step, carry):
        square_copy(step).start()
        return carry

    lax.fori_loop(1, total, send_squares, 0)

    @pl.when(row < rows - 1)
    def _():
        for copy in halo_copies:
            copy.start()

    sq_slots[me] = sq_send[...]

    lax.fori_loop(
        own, panels, lambda n, carry: choose(lax.rem(col * own + n, panels), carry), 0
    )
    for copy in in_copies:
        copy.wait()

    for b in range(block_count):
        hmat[b, 0] = coup_ref[b].astype(jnp.bfloat16)
        hmat[b, 1] = (0.5 * diag_ref[b]).astype(jnp.bfloat16)
        onsite_col[b * block : (b + 1) * block, :] = column_form(
            0.5 * onsite_ref[0:1, b * block : (b + 1) * block]
        )

    def await_squares(step, carry):
        other = lax.rem(me + step, total)
        square_copy(step).wait_send()
        pltpu.make_async_remote_copy(
            src_ref=sq_send,
            dst_ref=sq_slots.at[other],
            send_sem=sq_send_sem.at[step],
            recv_sem=sq_recv_sem.at[other],
            device_id=(other // cols, lax.rem(other, cols)),
            device_id_type=MESH,
        ).wait_recv()
        return carry

    lax.fori_loop(1, total, await_squares, 0)

    def make_factors(c):
        sums = lax.fori_loop(
            0, rows, lambda r, a: a + sq_slots[r * cols + c], jnp.zeros(sq_send.shape, jnp.float32)
        )
        factor = lax.rsqrt(sums + EPSILON)
        for k in range(own):
            factor_col[c * own + k] = column_form(
                jnp.concatenate(
                    [factor[k * sub + t : k * sub + t + 1, :] for t in range(sub)], axis=1
                )
            )

    def form_block(poles, weight_row, group, q_block, store):
        scaled = [
            cauchy_of(poles, weight_row, group * own + k) * widen(factor_col[group * own + k], block)
            for k in range(own)
        ]
        scaled = jnp.concatenate([part.astype(jnp.bfloat16) for part in scaled], axis=0)
        result = dot_nt(scaled, q_block).astype(jnp.bfloat16)
        for k in range(own):
            store(k, result[k * size : (k + 1) * size])

    def form_group(group):
        make_factors(group)
        for b in range(block_count):
            lanes = pl.ds(b * block, block)

            def store(k, value):
                formed[group * own + k, :, lanes] = value

            form_block(pw[0:1, lanes], pw[8:9, lanes], group, q_ref[b], store)

    form_group(col)

    @pl.when(row > 0)
    def _():
        for copy in halo_copies:
            copy.wait_recv()

        def store(k, value):
            halo[k] = value

        form_block(halo_pw[0:1, :], halo_pw[8:9, :], col, halo_q[...], store)

    @pl.when(row == 0)
    def _():
        halo[...] = jnp.zeros_like(halo)

    def plane_copy(k, source_low):
        return pltpu.make_async_remote_copy(
            src_ref=sums_send.at[k],
            dst_ref=plane_slots.at[k, source_low],
            send_sem=plane_send_sem.at[k],
            recv_sem=plane_recv_sem.at[k, source_low],
            device_id=(collector, col),
            device_id_type=MESH,
        )

    def sums_copy(k, source_high):
        return pltpu.make_async_remote_copy(
            src_ref=sums_send.at[k],
            dst_ref=sums_slots.at[source_high],
            send_sem=sums_send_sem.at[k],
            recv_sem=sums_recv_sem.at[source_high],
            device_id=(k * spread + low_row, col),
            device_id_type=MESH,
        )

    def collect(k):
        def add(step, carry):
            other = lax.rem(low_row + step, spread)
            plane_copy(k, other).wait_recv()
            sums_send[k] += plane_slots[k, other]
            return carry

        lax.fori_loop(1, spread, add, 0)

        @pl.when(high_row != k)
        def _():
            sums_copy(k, high_row).start()

    def own_panel(k, carry):
        panel = col * own + k
        gram = jnp.zeros((size, size), jnp.float32)
        half = jnp.zeros((size, size), jnp.float32)
        before = jnp.transpose(halo[k])
        for b in range(block_count):
            lanes = pl.ds(b * block, block)
            now = formed[panel, :, lanes]
            now_turned = jnp.transpose(now)
            image = jnp.dot(hmat[b, 0], before, preferred_element_type=jnp.float32)
            image = image + jnp.dot(hmat[b, 1], now_turned, preferred_element_type=jnp.float32)
            onsite = widen(onsite_col[b * block : (b + 1) * block, :], size)
            image = image + onsite * now_turned.astype(jnp.float32)
            high, low = split(image)
            gram = gram + jnp.dot(now, now_turned, preferred_element_type=jnp.float32)
            half = half + jnp.dot(now, high, preferred_element_type=jnp.float32)
            half = half + jnp.dot(now, low, preferred_element_type=jnp.float32)
            before = now_turned
        projected = half + jnp.transpose(half)
        sums_send[k, 0:size, :] = jnp.where(j_at > i_at, gram, projected)
        diagonal = jnp.sum(jnp.where(i_at == j_at, gram, 0.0), axis=0, keepdims=True)
        sums_send[k, size : size + 8, :] = jnp.broadcast_to(diagonal, (8, size))

        @pl.when(jnp.logical_not(collects))
        def _():
            plane_copy(k, low_row).start()

        @pl.when(jnp.logical_and(collects, k > 0))
        def _():
            collect(k - 1)

        return carry

    lax.fori_loop(0, own, own_panel, 0)

    @pl.when(collects)
    def _():
        collect(own - 1)

    def form_rest(n, carry):
        form_group(lax.rem(col + n, cols))
        return carry

    late = max(1, cols - 1)
    lax.fori_loop(1, late, form_rest, 0)

    def relay_copy(step):
        other = lax.rem(high_row + step, own)
        return pltpu.make_async_remote_copy(
            src_ref=relay.at[high_row],
            dst_ref=relay.at[high_row],
            send_sem=relay_send_sem.at[step],
            recv_sem=relay_recv_sem.at[high_row],
            device_id=(other * spread + low_row, col),
            device_id_type=MESH,
        )

    def update_copy(k, step):
        other = lax.rem(low_row * cols + col + step, spread * cols)
        other_col = lax.rem(other, cols)
        return pltpu.make_async_remote_copy(
            src_ref=relay.at[k, other_col],
            dst_ref=update_out.at[col * own + k],
            send_sem=v_send_sem.at[k, step],
            recv_sem=v_recv_sem.at[col * own + k],
            device_id=(high_row * spread + other // cols, other_col),
            device_id_type=MESH,
        )

    def forward(k):
        def send_update(step, carry):
            update_copy(k, step).start()
            return carry

        lax.fori_loop(1, spread * cols, send_update, 0)
        update_out[col * own + k] = relay[k, col]

    @pl.when(collects)
    def _():
        panel = col * own + high_row

        def arrive(step, total_sums):
            other = lax.rem(high_row + step, own)
            sums_copy(high_row, other).wait_recv()
            return total_sums + sums_slots[other]

        sums = lax.fori_loop(1, own, arrive, sums_send[high_row])
        packed = sums[0:size, :]
        diagonal = sums[size : size + 1, :]
        turned = jnp.transpose(packed)
        on_diagonal = i_at == j_at
        identity = jnp.where(on_diagonal, 1.0, 0.0)
        gram = jnp.where(j_at > i_at, packed, jnp.where(on_diagonal, diagonal, turned))
        projected = jnp.where(j_at > i_at, turned, packed)
        residual = identity - gram
        right = jnp.transpose(chosen_col_ref[panel])[0:1, :]
        left = widen(chosen_col_ref[panel], size)
        spacing = right - left + identity
        update = jnp.where(
            on_diagonal, 0.5 * residual, (projected + right * residual) / spacing
        )
        v = identity + update
        gv = jnp.dot(gram, v, precision=HIGHEST, preferred_element_type=jnp.float32)
        column_sums = jnp.sum(v * gv, axis=0, keepdims=True)
        matrix_order = float(here * rows)
        v = v * jnp.sqrt(matrix_order / column_sums)
        v_full[...] = jnp.transpose(v)
        new_roots = (
            jnp.sum(jnp.where(on_diagonal, projected, 0.0), axis=0, keepdims=True) / diagonal
        )
        for c in range(cols):
            lanes = slice(c * width, (c + 1) * width)
            relay[high_row, c, 0:width, :] = v_full[lanes, :]
            relay[high_row, c, width : width + 8, 0:width] = jnp.broadcast_to(
                new_roots[:, lanes], (8, width)
            )
        for step in range(1, own):
            relay_copy(step).start()
        forward(high_row)

    lax.fori_loop(late, cols, form_rest, 0)

    @pl.when(collects)
    def _():
        def pass_on(step, carry):
            k = lax.rem(high_row + step, own)
            pltpu.make_async_remote_copy(
                src_ref=relay.at[k],
                dst_ref=relay.at[k],
                send_sem=relay_send_sem.at[step],
                recv_sem=relay_recv_sem.at[k],
                device_id=(k * spread + low_row, col),
                device_id_type=MESH,
            ).wait_recv()
            forward(k)
            return carry

        lax.fori_loop(1, own, pass_on, 0)

    def out_copy(n):
        panel = lax.rem(n, cols) * own + lax.rem(high_row + n // cols, own)
        return pltpu.make_async_copy(
            stage.at[lax.rem(n, own)], refined_hbm.at[panel], out_sem.at[lax.rem(n, own)]
        )

    def finish(n, carry):
        c, k = lax.rem(n, cols), lax.rem(high_row + n // cols, own)
        panel = c * own + k
        from_row = high_row * spread + lax.rem(c, spread)

        @pl.when(jnp.logical_or(row != from_row, col != c))
        def _():
            pltpu.make_async_remote_copy(
                src_ref=relay.at[0, 0],
                dst_ref=update_out.at[panel],
                send_sem=v_send_sem.at[0, 0],
                recv_sem=v_recv_sem.at[panel],
                device_id=(from_row, c),
                device_id_type=MESH,
            ).wait_recv()

        high, low = split(update_out[panel, 0:width, :])
        parts = jnp.dot(
            jnp.concatenate([high, low], axis=0),
            formed[panel],
            preferred_element_type=jnp.float32,
        )
        roots_out[pl.ds(panel, 1), :] = update_out[panel, width : width + 1, 0:width]

        @pl.when(n >= own)
        def _():
            out_copy(n - own).wait()

        stage[lax.rem(n, own)] = parts[0:width] + parts[width : 2 * width]
        out_copy(n).start()
        return carry

    lax.fori_loop(0, panels, finish, 0)

    @pl.when(collects)
    def _():
        def sent(n, carry):
            update_copy(n // (spread * cols - 1), 1 + lax.rem(n, spread * cols - 1)).wait_send()
            return carry

        lax.fori_loop(0, own * (spread * cols - 1), sent, 0)
        for step in range(1, own):
            relay_copy(step).wait_send()
        for k in range(own):

            @pl.when(high_row != k)
            def _():
                sums_copy(k, high_row).wait_send()

    @pl.when(jnp.logical_not(collects))
    def _():
        for k in range(own):
            plane_copy(k, low_row).wait_send()

    @pl.when(row < rows - 1)
    def _():
        for copy in halo_copies:
            copy.wait_send()

    def written(n, carry):
        out_copy(n).wait()
        return carry

    lax.fori_loop(panels - own, panels, written, 0)


def shards(
    pole_values,
    rank_one,
    deflated,
    onsite_energy,
    secular_roots,
    column_order,
    q_blocks,
    diag_blocks,
    coupling_blocks,
):
    rows, cols = lax.axis_size("row"), lax.axis_size("col")
    here = pole_values.shape[0]
    panels, size = secular_roots.shape
    block_count, block, _ = q_blocks.shape
    width = size // cols
    own = panels // cols
    total = rows * cols
    spread = rows // own
    sub = size // LANES
    squares_pad = -(-own * sub // 8) * 8
    vmem = pl.BlockSpec(memory_space=pltpu.VMEM)
    f32, bf16 = jnp.float32, jnp.bfloat16
    dma = pltpu.SemaphoreType.DMA
    anywhere = pl.BlockSpec(memory_space=pl.ANY)
    refined, new_roots = pl.pallas_call(
        functools.partial(merge_kernel, rows, cols),
        out_shape=(
            jax.ShapeDtypeStruct((panels, width, here), f32),
            jax.ShapeDtypeStruct((panels, width), f32),
        ),
        in_specs=[vmem] * 6 + [anywhere] * 3,
        out_specs=(anywhere, vmem),
        scratch_shapes=[
            pltpu.VMEM(q_blocks.shape, bf16),
            pltpu.VMEM(diag_blocks.shape, f32),
            pltpu.VMEM(coupling_blocks.shape, f32),
            pltpu.VMEM((panels, size, LANES), f32),
            pltpu.VMEM((panels, width + 8, size), f32),
            pltpu.VMEM((own, width, here), f32),
            pltpu.VMEM((16, here), f32),
            pltpu.VMEM((16, block), f32),
            pltpu.VMEM((block, block), bf16),
            pltpu.VMEM((squares_pad, LANES), f32),
            pltpu.VMEM((total, squares_pad, LANES), f32),
            pltpu.VMEM((panels, size, LANES), f32),
            pltpu.VMEM((block_count, 2, block, block), bf16),
            pltpu.VMEM((here, LANES), f32),
            pltpu.VMEM((panels, size, here), bf16),
            pltpu.VMEM((own, size, block), bf16),
            pltpu.VMEM((own, size + 8, size), f32),
            pltpu.VMEM((own, spread, size + 8, size), f32),
            pltpu.VMEM((own, size + 8, size), f32),
            pltpu.VMEM((size, size), f32),
            pltpu.VMEM((own, cols, width + 8, size), f32),
            dma((3,)),
            dma((own,)),
            dma((2,)),
            dma((2,)),
            dma((total,)),
            dma((total,)),
            dma((own,)),
            dma((own, spread)),
            dma((own,)),
            dma((own,)),
            dma((own,)),
            dma((own,)),
            dma((own, spread * cols)),
            dma((panels,)),
        ],
        compiler_params=pltpu.CompilerParams(
            collective_id=0, has_side_effects=True, vmem_limit_bytes=60 * 2**20
        ),
        name="merge",
    )(
        pole_values.reshape(1, here),
        rank_one.reshape(1, here),
        deflated.reshape(1, here),
        onsite_energy.reshape(1, here),
        secular_roots,
        column_order,
        q_blocks,
        diag_blocks,
        coupling_blocks,
    )
    return (jnp.swapaxes(refined, 1, 2), new_roots)


def solution(mesh):
    placed = (
        P("row"),
        P("row"),
        P("row"),
        P("row"),
        P(),
        P(),
        P("row", None, None),
        P("row", None, None),
        P("row", None, None),
    )
    return jax.shard_map(
        shards,
        mesh=mesh,
        in_specs=placed,
        out_specs=(P(None, "row", "col"), P(None, "col")),
        check_vma=False,
    )
```

```python
import functools

import jax
import jax.numpy as jnp
from jax import lax
from jax.experimental import pallas as pl
from jax.experimental.pallas import tpu as pltpu
from jax.sharding import PartitionSpec as P

EPSILON = 1e-06
HIGHEST = lax.Precision.HIGHEST
MESH = pl.DeviceIdType.MESH
LANES = 128


def dot_nt(a, b):
    return lax.dot_general(a, b, (((1,), (1,)), ((), ())), preferred_element_type=jnp.float32)


def split(x):
    high = x.astype(jnp.bfloat16)
    return high, (x - high.astype(jnp.float32)).astype(jnp.bfloat16)


def widen(x, width):
    return jnp.concatenate([x] * (width // x.shape[1]), axis=1)


def column_form(row):
    return jnp.transpose(jnp.broadcast_to(row, (LANES, row.shape[1])))


def merge_kernel(
    rows,
    cols,
    pole_ref,
    rank_ref,
    defl_ref,
    onsite_ref,
    roots_ref,
    order_ref,
    q_hbm,
    diag_hbm,
    coup_hbm,
    refined_hbm,
    roots_out,
    q_ref,
    diag_ref,
    coup_ref,
    chosen_col_ref,
    update_out,
    stage,
    pw,
    halo_pw,
    halo_q,
    sq_send,
    sq_slots,
    factor_col,
    hmat,
    onsite_col,
    formed,
    halo,
    sums_send,
    plane_slots,
    sums_slots,
    v_full,
    relay,
    in_sem,
    out_sem,
    halo_send_sem,
    halo_recv_sem,
    sq_send_sem,
    sq_recv_sem,
    plane_send_sem,
    plane_recv_sem,
    sums_send_sem,
    sums_recv_sem,
    relay_send_sem,
    relay_recv_sem,
    v_send_sem,
    v_recv_sem,
):
    row = lax.axis_index("row")
    col = lax.axis_index("col")
    me = row * cols + col
    total = rows * cols
    panels, size = roots_ref.shape
    own = panels // cols
    block_count, block, _ = q_ref.shape
    here = block_count * block
    width = size // cols
    spread = rows // own
    sub = size // LANES
    high_row, low_row = row // spread, lax.rem(row, spread)
    collects = low_row == lax.rem(col, spread)
    collector = high_row * spread + lax.rem(col, spread)

    in_copies = [
        pltpu.make_async_copy(source, target, in_sem.at[n])
        for n, (source, target) in enumerate(
            ((q_hbm, q_ref), (coup_hbm, coup_ref), (diag_hbm, diag_ref))
        )
    ]
    for copy in in_copies:
        copy.start()

    barrier = pltpu.get_barrier_semaphore()

    def greet(step, carry):
        other = lax.rem(me + step, total)
        pl.semaphore_signal(
            barrier, inc=1, device_id=(other // cols, lax.rem(other, cols)), device_id_type=MESH
        )
        return carry

    lax.fori_loop(1, total, greet, 0)

    weights = rank_ref[...] * (1 - defl_ref[...]).astype(jnp.float32)
    pw[0:8, :] = jnp.broadcast_to(pole_ref[...], (8, here))
    pw[8:16, :] = jnp.broadcast_to(weights, (8, here))

    i_at = lax.broadcasted_iota(jnp.int32, (size, size), 0)
    j_at = lax.broadcasted_iota(jnp.int32, (size, size), 1)

    def choose(panel, carry=0):
        order = column_form(order_ref[pl.ds(panel, 1), :].astype(jnp.float32))
        selector = jnp.where(widen(order, size) == j_at.astype(jnp.float32), 1.0, 0.0)
        selector = selector.astype(jnp.bfloat16)
        roots = column_form(roots_ref[pl.ds(panel, 1), :])
        high, low = split(roots)
        rest = (roots - high.astype(jnp.float32)) - low.astype(jnp.float32)
        picked = [
            jnp.dot(selector, part, preferred_element_type=jnp.float32)
            for part in (high, low, rest.astype(jnp.bfloat16))
        ]
        chosen_col_ref[panel] = (picked[0] + picked[1]) + picked[2]
        return carry

    def cauchy_of(poles, weight_row, panel):
        chosen = widen(chosen_col_ref[panel], poles.shape[1])
        return weight_row / (poles - chosen)

    sq_send[...] = jnp.zeros_like(sq_send)
    for k in range(own):
        choose(col * own + k)

        def add_squares(b, acc):
            lanes = pl.ds(pl.multiple_of(b * block, block), block)
            c = cauchy_of(pw[0:1, lanes], pw[8:9, lanes], col * own + k)
            c = c * c
            for t in range(block // LANES):
                acc = acc + c[:, t * LANES : (t + 1) * LANES]
            return acc

        acc = lax.fori_loop(0, block_count, add_squares, jnp.zeros((size, LANES), jnp.float32))
        squares = jnp.sum(jnp.transpose(acc), axis=0, keepdims=True)
        for t in range(sub):
            sq_send[k * sub + t : k * sub + t + 1, :] = squares[:, t * LANES : (t + 1) * LANES]

    pl.semaphore_wait(barrier, total - 1)

    last = block_count - 1
    tail = pl.ds(here - block, block)
    halo_copies = [
        pltpu.make_async_remote_copy(
            src_ref=source,
            dst_ref=target,
            send_sem=halo_send_sem.at[n],
            recv_sem=halo_recv_sem.at[n],
            device_id=(lax.rem(row + 1, rows), col),
            device_id_type=MESH,
        )
        for n, (source, target) in enumerate(((q_hbm.at[last], halo_q), (pw.at[:, tail], halo_pw)))
    ]

    def square_copy(step):
        other = lax.rem(me + step, total)
        return pltpu.make_async_remote_copy(
            src_ref=sq_send,
            dst_ref=sq_slots.at[me],
            send_sem=sq_send_sem.at[step],
            recv_sem=sq_recv_sem.at[me],
            device_id=(other // cols, lax.rem(other, cols)),
            device_id_type=MESH,
        )

    def send_squares(step, carry):
        square_copy(step).start()
        return carry

    lax.fori_loop(1, total, send_squares, 0)

    @pl.when(row < rows - 1)
    def _():
        for copy in halo_copies:
            copy.start()

    sq_slots[me] = sq_send[...]

    lax.fori_loop(
        own, panels, lambda n, carry: choose(lax.rem(col * own + n, panels), carry), 0
    )
    for copy in in_copies:
        copy.wait()

    for b in range(block_count):
        hmat[b, 0] = coup_ref[b].astype(jnp.bfloat16)
        hmat[b, 1] = (0.5 * diag_ref[b]).astype(jnp.bfloat16)
        onsite_col[b * block : (b + 1) * block, :] = column_form(
            0.5 * onsite_ref[0:1, b * block : (b + 1) * block]
        )

    def await_squares(step, carry):
        other = lax.rem(me + step, total)
        square_copy(step).wait_send()
        pltpu.make_async_remote_copy(
            src_ref=sq_send,
            dst_ref=sq_slots.at[other],
            send_sem=sq_send_sem.at[step],
            recv_sem=sq_recv_sem.at[other],
            device_id=(other // cols, lax.rem(other, cols)),
            device_id_type=MESH,
        ).wait_recv()
        return carry

    lax.fori_loop(1, total, await_squares, 0)

    def make_factors(c):
        sums = lax.fori_loop(
            0, rows, lambda r, a: a + sq_slots[r * cols + c], jnp.zeros(sq_send.shape, jnp.float32)
        )
        factor = lax.rsqrt(sums + EPSILON)
        for k in range(own):
            factor_col[c * own + k] = column_form(
                jnp.concatenate(
                    [factor[k * sub + t : k * sub + t + 1, :] for t in range(sub)], axis=1
                )
            )

    def form_block(poles, weight_row, group, q_block, store):
        scaled = [
            cauchy_of(poles, weight_row, group * own + k) * widen(factor_col[group * own + k], block)
            for k in range(own)
        ]
        scaled = jnp.concatenate([part.astype(jnp.bfloat16) for part in scaled], axis=0)
        result = dot_nt(scaled, q_block).astype(jnp.bfloat16)
        for k in range(own):
            store(k, result[k * size : (k + 1) * size])

    def form_group(group):
        make_factors(group)
        for b in range(block_count):
            lanes = pl.ds(b * block, block)

            def store(k, value):
                formed[group * own + k, :, lanes] = value

            form_block(pw[0:1, lanes], pw[8:9, lanes], group, q_ref[b], store)

    form_group(col)

    @pl.when(row > 0)
    def _():
        for copy in halo_copies:
            copy.wait_recv()

        def store(k, value):
            halo[k] = value

        form_block(halo_pw[0:1, :], halo_pw[8:9, :], col, halo_q[...], store)

    @pl.when(row == 0)
    def _():
        halo[...] = jnp.zeros_like(halo)

    def plane_copy(k, source_low):
        return pltpu.make_async_remote_copy(
            src_ref=sums_send.at[k],
            dst_ref=plane_slots.at[k, source_low],
            send_sem=plane_send_sem.at[k],
            recv_sem=plane_recv_sem.at[k, source_low],
            device_id=(collector, col),
            device_id_type=MESH,
        )

    def sums_copy(k, source_high):
        return pltpu.make_async_remote_copy(
            src_ref=sums_send.at[k],
            dst_ref=sums_slots.at[source_high],
            send_sem=sums_send_sem.at[k],
            recv_sem=sums_recv_sem.at[source_high],
            device_id=(k * spread + low_row, col),
            device_id_type=MESH,
        )

    def collect(k):
        def add(step, carry):
            other = lax.rem(low_row + step, spread)
            plane_copy(k, other).wait_recv()
            sums_send[k] += plane_slots[k, other]
            return carry

        lax.fori_loop(1, spread, add, 0)

        @pl.when(high_row != k)
        def _():
            sums_copy(k, high_row).start()

    def own_panel(step, carry):
        k = lax.rem(high_row + 1 + step, own)
        panel = col * own + k
        gram = jnp.zeros((size, size), jnp.float32)
        half = jnp.zeros((size, size), jnp.float32)
        before = jnp.transpose(halo[k])
        for b in range(block_count):
            lanes = pl.ds(b * block, block)
            now = formed[panel, :, lanes]
            now_turned = jnp.transpose(now)
            image = jnp.dot(hmat[b, 0], before, preferred_element_type=jnp.float32)
            image = image + jnp.dot(hmat[b, 1], now_turned, preferred_element_type=jnp.float32)
            onsite = widen(onsite_col[b * block : (b + 1) * block, :], size)
            image = image + onsite * now_turned.astype(jnp.float32)
            high, low = split(image)
            gram = gram + jnp.dot(now, now_turned, preferred_element_type=jnp.float32)
            half = half + jnp.dot(now, high, preferred_element_type=jnp.float32)
            half = half + jnp.dot(now, low, preferred_element_type=jnp.float32)
            before = now_turned
        projected = half + jnp.transpose(half)
        sums_send[k, 0:size, :] = jnp.where(j_at > i_at, gram, projected)
        diagonal = jnp.sum(jnp.where(i_at == j_at, gram, 0.0), axis=0, keepdims=True)
        sums_send[k, size : size + 8, :] = jnp.broadcast_to(diagonal, (8, size))

        @pl.when(jnp.logical_not(collects))
        def _():
            plane_copy(k, low_row).start()

        @pl.when(jnp.logical_and(collects, step > 0))
        def _():
            collect(lax.rem(high_row + step, own))

        return carry

    lax.fori_loop(0, own, own_panel, 0)

    def form_rest(n, carry):
        form_group(lax.rem(col + n, cols))
        return carry

    late = min(2, cols)
    lax.fori_loop(1, late, form_rest, 0)

    def relay_copy(step):
        other = lax.rem(high_row + step, own)
        return pltpu.make_async_remote_copy(
            src_ref=relay.at[high_row],
            dst_ref=relay.at[high_row],
            send_sem=relay_send_sem.at[step],
            recv_sem=relay_recv_sem.at[high_row],
            device_id=(other * spread + low_row, col),
            device_id_type=MESH,
        )

    def update_copy(k, step):
        other = lax.rem(low_row * cols + col + step, spread * cols)
        other_col = lax.rem(other, cols)
        return pltpu.make_async_remote_copy(
            src_ref=relay.at[k, other_col],
            dst_ref=update_out.at[col * own + k],
            send_sem=v_send_sem.at[k, step],
            recv_sem=v_recv_sem.at[col * own + k],
            device_id=(high_row * spread + other // cols, other_col),
            device_id_type=MESH,
        )

    def forward(k):
        def send_update(step, carry):
            update_copy(k, step).start()
            return carry

        lax.fori_loop(1, spread * cols, send_update, 0)
        update_out[col * own + k] = relay[k, col]

    @pl.when(collects)
    def _():
        panel = col * own + high_row
        collect(high_row)

        def arrive(step, total_sums):
            other = lax.rem(high_row + step, own)
            sums_copy(high_row, other).wait_recv()
            return total_sums + sums_slots[other]

        sums = lax.fori_loop(1, own, arrive, sums_send[high_row])
        packed = sums[0:size, :]
        diagonal = sums[size : size + 1, :]
        turned = jnp.transpose(packed)
        on_diagonal = i_at == j_at
        identity = jnp.where(on_diagonal, 1.0, 0.0)
        gram = jnp.where(j_at > i_at, packed, jnp.where(on_diagonal, diagonal, turned))
        projected = jnp.where(j_at > i_at, turned, packed)
        residual = identity - gram
        right = jnp.transpose(chosen_col_ref[panel])[0:1, :]
        left = widen(chosen_col_ref[panel], size)
        spacing = right - left + identity
        update = jnp.where(
            on_diagonal, 0.5 * residual, (projected + right * residual) / spacing
        )
        v = identity + update
        gv = jnp.dot(gram, v, precision=HIGHEST, preferred_element_type=jnp.float32)
        column_sums = jnp.sum(v * gv, axis=0, keepdims=True)
        matrix_order = float(here * rows)
        v = v * jnp.sqrt(matrix_order / column_sums)
        v_full[...] = jnp.transpose(v)
        new_roots = (
            jnp.sum(jnp.where(on_diagonal, projected, 0.0), axis=0, keepdims=True) / diagonal
        )
        for c in range(cols):
            lanes = slice(c * width, (c + 1) * width)
            relay[high_row, c, 0:width, :] = v_full[lanes, :]
            relay[high_row, c, width : width + 8, 0:width] = jnp.broadcast_to(
                new_roots[:, lanes], (8, width)
            )
        for step in range(1, own):
            relay_copy(step).start()
        forward(high_row)

    def pass_on(step, carry):
        k = lax.rem(high_row + step, own)
        pltpu.make_async_remote_copy(
            src_ref=relay.at[k],
            dst_ref=relay.at[k],
            send_sem=relay_send_sem.at[step],
            recv_sem=relay_recv_sem.at[k],
            device_id=(k * spread + low_row, col),
            device_id_type=MESH,
        ).wait_recv()
        forward(k)
        return carry

    def form_and_pass(n, carry):
        form_rest(n, carry)

        @pl.when(jnp.logical_and(collects, n - late + 1 < own))
        def _():
            pass_on(n - late + 1, 0)

        return carry

    lax.fori_loop(late, cols, form_and_pass, 0)

    @pl.when(collects)
    def _():
        lax.fori_loop(min(own, 1 + cols - late), own, pass_on, 0)

    def out_copy(n):
        panel = lax.rem(n, cols) * own + lax.rem(high_row + n // cols, own)
        return pltpu.make_async_copy(
            stage.at[lax.rem(n, own)], refined_hbm.at[panel], out_sem.at[lax.rem(n, own)]
        )

    def finish(n, carry):
        c, k = lax.rem(n, cols), lax.rem(high_row + n // cols, own)
        panel = c * own + k
        from_row = high_row * spread + lax.rem(c, spread)

        @pl.when(jnp.logical_or(row != from_row, col != c))
        def _():
            pltpu.make_async_remote_copy(
                src_ref=relay.at[0, 0],
                dst_ref=update_out.at[panel],
                send_sem=v_send_sem.at[0, 0],
                recv_sem=v_recv_sem.at[panel],
                device_id=(from_row, c),
                device_id_type=MESH,
            ).wait_recv()

        high, low = split(update_out[panel, 0:width, :])
        parts = jnp.dot(
            jnp.concatenate([high, low], axis=0),
            formed[panel],
            preferred_element_type=jnp.float32,
        )
        roots_out[pl.ds(panel, 1), :] = update_out[panel, width : width + 1, 0:width]

        @pl.when(n >= own)
        def _():
            out_copy(n - own).wait()

        stage[lax.rem(n, own)] = parts[0:width] + parts[width : 2 * width]
        out_copy(n).start()
        return carry

    lax.fori_loop(0, panels, finish, 0)

    @pl.when(collects)
    def _():
        def sent(n, carry):
            update_copy(n // (spread * cols - 1), 1 + lax.rem(n, spread * cols - 1)).wait_send()
            return carry

        lax.fori_loop(0, own * (spread * cols - 1), sent, 0)
        for step in range(1, own):
            relay_copy(step).wait_send()
        for k in range(own):

            @pl.when(high_row != k)
            def _():
                sums_copy(k, high_row).wait_send()

    @pl.when(jnp.logical_not(collects))
    def _():
        for k in range(own):
            plane_copy(k, low_row).wait_send()

    @pl.when(row < rows - 1)
    def _():
        for copy in halo_copies:
            copy.wait_send()

    def written(n, carry):
        out_copy(n).wait()
        return carry

    lax.fori_loop(panels - own, panels, written, 0)


def shards(
    pole_values,
    rank_one,
    deflated,
    onsite_energy,
    secular_roots,
    column_order,
    q_blocks,
    diag_blocks,
    coupling_blocks,
):
    rows, cols = lax.axis_size("row"), lax.axis_size("col")
    here = pole_values.shape[0]
    panels, size = secular_roots.shape
    block_count, block, _ = q_blocks.shape
    width = size // cols
    own = panels // cols
    total = rows * cols
    spread = rows // own
    sub = size // LANES
    squares_pad = -(-own * sub // 8) * 8
    vmem = pl.BlockSpec(memory_space=pltpu.VMEM)
    f32, bf16 = jnp.float32, jnp.bfloat16
    dma = pltpu.SemaphoreType.DMA
    anywhere = pl.BlockSpec(memory_space=pl.ANY)
    refined, new_roots = pl.pallas_call(
        functools.partial(merge_kernel, rows, cols),
        out_shape=(
            jax.ShapeDtypeStruct((panels, width, here), f32),
            jax.ShapeDtypeStruct((panels, width), f32),
        ),
        in_specs=[vmem] * 6 + [anywhere] * 3,
        out_specs=(anywhere, vmem),
        scratch_shapes=[
            pltpu.VMEM(q_blocks.shape, bf16),
            pltpu.VMEM(diag_blocks.shape, f32),
            pltpu.VMEM(coupling_blocks.shape, f32),
            pltpu.VMEM((panels, size, LANES), f32),
            pltpu.VMEM((panels, width + 8, size), f32),
            pltpu.VMEM((own, width, here), f32),
            pltpu.VMEM((16, here), f32),
            pltpu.VMEM((16, block), f32),
            pltpu.VMEM((block, block), bf16),
            pltpu.VMEM((squares_pad, LANES), f32),
            pltpu.VMEM((total, squares_pad, LANES), f32),
            pltpu.VMEM((panels, size, LANES), f32),
            pltpu.VMEM((block_count, 2, block, block), bf16),
            pltpu.VMEM((here, LANES), f32),
            pltpu.VMEM((panels, size, here), bf16),
            pltpu.VMEM((own, size, block), bf16),
            pltpu.VMEM((own, size + 8, size), f32),
            pltpu.VMEM((own, spread, size + 8, size), f32),
            pltpu.VMEM((own, size + 8, size), f32),
            pltpu.VMEM((size, size), f32),
            pltpu.VMEM((own, cols, width + 8, size), f32),
            dma((3,)),
            dma((own,)),
            dma((2,)),
            dma((2,)),
            dma((total,)),
            dma((total,)),
            dma((own,)),
            dma((own, spread)),
            dma((own,)),
            dma((own,)),
            dma((own,)),
            dma((own,)),
            dma((own, spread * cols)),
            dma((panels,)),
        ],
        compiler_params=pltpu.CompilerParams(
            collective_id=0, has_side_effects=True, vmem_limit_bytes=60 * 2**20
        ),
        name="merge",
    )(
        pole_values.reshape(1, here),
        rank_one.reshape(1, here),
        deflated.reshape(1, here),
        onsite_energy.reshape(1, here),
        secular_roots,
        column_order,
        q_blocks,
        diag_blocks,
        coupling_blocks,
    )
    return (jnp.swapaxes(refined, 1, 2), new_roots)


def solution(mesh):
    placed = (
        P("row"),
        P("row"),
        P("row"),
        P("row"),
        P(),
        P(),
        P("row", None, None),
        P("row", None, None),
        P("row", None, None),
    )
    return jax.shard_map(
        shards,
        mesh=mesh,
        in_specs=placed,
        out_specs=(P(None, "row", "col"), P(None, "col")),
        check_vma=False,
    )
```
